256 devices in a mesh: layer: 32 (over x, z), row: 8 (over y, core).
Axes of the slice: x: 4, y: 4, z: 8, core: 2. Of those that a mesh axis runs over, the one named last changes fastest.
Arguments:
- leaf_rhs: bfloat16 [262144, 512], P(('layer', 'row')), may hold values from -3 to 3
- leaf_inv: bfloat16 [2048, 128, 128], P(('layer', 'row')), may hold values from -1 to 1.25, as said below
- coupling: bfloat16 [262144, 5, 128], P(('layer', 'row')), may hold values from -0.046875 to 0.046875
- pattern: int32 [2048, 5], P(('layer', 'row')), may hold values 0 or 1
- anc_rhs: float32 [32, 5, 1024, 512], P('layer', None, 'row'), may hold values from -2 to 2
- anc_blocks: bfloat16 [32, 15, 1024, 1024], P('layer', None, 'row'), may hold values from -1 to 1.25, as said below
Outputs:
- x_leaf: float32 [262144, 512], P(('layer', 'row'))
- x_anc: float32 [32, 5, 1024, 512], P('layer', None, 'row')
The draws below stay inside these ranges and needn't reach their ends.
Inputs may be any that keep to these rules, and one draw needn't show every extreme that they name: `leaf_inv`: each block is lower triangular with a positive diagonal. For every level t and block index k of blk(s, t), the copies anc_blocks[l, k] are equal for all layers l of one group of 2 ** (t + 1) layers; the blocks blk(t, t) are lower triangular with a positive diagonal.
All inputs are finite; a program needn't handle non-finite values. No bound on the sum of `pattern` on one device may be relied on, other than what follows from the above.
Results may differ from the reference program's by a relative error of at most 0.009.
Values may be sent and summed in bfloat16 or wider, within the bound.
No kernel may reach another device: no remote copies, remote signals or barrier semaphores. Data moves between devices by JAX's collectives and lax.ppermute only.
A program may use at most 64 MiB of HBM per device.

```python
import math
import jax
import jax.numpy as jnp
from jax import lax

B = 128
R = 512
ANC = 1024
SN_DEV = 8
LEVELS = 5
ANC_DEV = 128
LEAF_SN = 2048
LEAF_ROWS = 262144
N_LAYER = 32
N_ROW = 8


def lower_inverse(key, block_count, block_order):
    key_diagonal, key_lower = jax.random.split(key)
    row_ids = jnp.arange(block_order)[:, None]
    column_ids = jnp.arange(block_order)[None, :]
    below_mask = (row_ids > column_ids).astype(jnp.float32)
    diagonal_part = jax.random.uniform(key_diagonal, (block_count, block_order), jnp.float32, 0.6, 1.2)
    lower_part = jnp.clip(jax.random.normal(key_lower, (block_count, block_order, block_order), jnp.float32), -4.0, 4.0)
    lower_part = lower_part * (0.5 / math.sqrt(block_order * 1.0)) * below_mask
    return lower_part + diagonal_part[:, :, None] * jnp.eye(block_order, dtype=jnp.float32)


def draw_leaf_inv(key, part):
    return lower_inverse(jax.random.fold_in(key, 11), LEAF_SN, B).astype(jnp.bfloat16)


def draw_anc_blocks(key, part):
    layer_total = 2 ** LEVELS
    blocks_out = []
    for tree_level in range(LEVELS):
        group_size = 2 ** (tree_level + 1)
        group_count = layer_total // group_size
        for above in range(tree_level, LEVELS):
            sub_key = jax.random.fold_in(jax.random.fold_in(key, 31 + tree_level), above)
            if above == tree_level:
                fresh = lower_inverse(sub_key, group_count, ANC)
            else:
                scale_value = 0.6 / math.sqrt(ANC * 2.0 ** (above - tree_level))
                fresh = jnp.clip(jax.random.normal(sub_key, (group_count, ANC, ANC), jnp.float32), -4.0, 4.0) * scale_value
            blocks_out.append(jnp.repeat(fresh.astype(jnp.bfloat16), group_size, axis=0))
    return jnp.stack(blocks_out, axis=1)


def draw_anc_rhs(key, part):
    sub_key = jax.random.fold_in(key, 57)
    shape_full = (2 ** LEVELS, LEVELS, ANC, R)
    scales = 0.5 * 2.0 ** (-(jnp.arange(LEVELS, dtype=jnp.float32) + 1.0) / 2.0)
    base_values = jnp.clip(jax.random.normal(sub_key, shape_full, jnp.float32), -4.0, 4.0)
    return base_values * scales[None, :, None, None]


def touch_ends(result, own_key, low, high):
    extent = result.shape
    spot = [jax.random.randint(jax.random.fold_in(own_key, axis), (), 0, extent[axis]) for axis in range(len(extent))]
    result = result.at[tuple(spot)].set(low)
    longest = extent.index(max(extent))
    spot[longest] = (spot[longest] + 1) % extent[longest]
    return result.at[tuple(spot)].set(high)


def block_levels(key, shape, shards, smallest, largest):
    loudness, own = 1.0, jax.random.fold_in(key, 6)
    for axis_at, parts in shards:
        heights = jnp.exp(jax.random.uniform(jax.random.fold_in(own, axis_at), (parts,), jnp.float32, smallest / len(shards), largest / len(shards)))
        loudness = loudness * jnp.repeat(heights, shape[axis_at] // parts).reshape([-1 if axis == axis_at else 1 for axis in range(len(shape))])
    return loudness


def scatter_about(own_key, extent, deviation, most, shards=(), kind=jnp.bfloat16):
    entries = deviation * jax.random.normal(own_key, extent, jnp.float32)
    if shards:
        entries = entries * block_levels(own_key, extent, shards, -0.22, 0.18)
    return jnp.clip(entries, -most, most).astype(kind)


def setup_inputs(seed: int = 0) -> dict:
    key_of = jax.random.split(jax.random.key(seed), 7)
    leaf_rhs = scatter_about(key_of[0], (LEAF_ROWS, R), 0.5, 3.0, ((0, 256),))
    leaf_inv = draw_leaf_inv(jax.random.fold_in(key_of[6], 71), 0)
    coupling = scatter_about(key_of[2], (LEAF_ROWS, LEVELS, ANC_DEV), (SN_DEV * B * N_LAYER // 2) ** -0.5, 0.046875, ((0, 256),))
    pattern = touch_ends((jax.random.randint(key_of[3], (LEAF_SN, LEVELS), 0, 4) < 3).astype(jnp.int32), jax.random.fold_in(key_of[3], 1), 0, 1)
    anc_rhs = draw_anc_rhs(jax.random.fold_in(key_of[6], 71), 0)
    anc_blocks = draw_anc_blocks(jax.random.fold_in(key_of[6], 71), 0)
    return dict(leaf_rhs=leaf_rhs, leaf_inv=leaf_inv, coupling=coupling, pattern=pattern, anc_rhs=anc_rhs, anc_blocks=anc_blocks)


def block_start(tree_level, level_total):
    return tree_level * level_total - tree_level * (tree_level - 1) // 2


def reference(leaf_rhs, leaf_inv, coupling, pattern, anc_rhs, anc_blocks):
    devices = N_LAYER * N_ROW
    rows_dev = SN_DEV * B
    right_dev = leaf_rhs.reshape(devices, SN_DEV, B, R)
    inverse_dev = leaf_inv.reshape(devices, SN_DEV, B, B)
    coupling_dev = coupling.reshape(devices, SN_DEV, B, LEVELS, ANC_DEV)
    pattern_dev = pattern.reshape(devices, SN_DEV, LEVELS)

    def masked_of(coupling_one, pattern_one):
        scaled = coupling_one * pattern_one.astype(jnp.bfloat16)[:, None, :, None]
        return scaled.reshape(rows_dev, LEVELS * ANC_DEV)

    def forward_leaf(operands):
        right_side, inverse, coupling_one, pattern_one = operands
        leaf_y = jnp.einsum("kab,kbr->kar", inverse.astype(jnp.float32), right_side.astype(jnp.float32))
        leaf_yb = leaf_y.astype(jnp.bfloat16).reshape(rows_dev, R)
        masked = masked_of(coupling_one, pattern_one)
        leaf_terms = jnp.dot(masked.T, leaf_yb, preferred_element_type=jnp.float32)
        return leaf_y, leaf_terms.reshape(LEVELS, ANC_DEV, R)

    leaf_y, leaf_terms = lax.map(forward_leaf, (right_dev, inverse_dev, coupling_dev, pattern_dev))
    leaf_terms = leaf_terms.reshape(N_LAYER, N_ROW, LEVELS, ANC_DEV, R)
    leaf_terms = leaf_terms.transpose(0, 2, 1, 3, 4).reshape(N_LAYER, LEVELS, ANC, R)
    share = anc_rhs - leaf_terms
    lowered = jnp.zeros((N_LAYER, LEVELS, ANC, R), jnp.float32)
    y_list = []
    for tree_level in range(LEVELS):
        group_size = 2 ** (tree_level + 1)
        group_count = N_LAYER // group_size
        level_total = (share[:, tree_level] - lowered[:, tree_level]).reshape(group_count, group_size, ANC, R).sum(axis=1)
        z_level = level_total.astype(jnp.bfloat16)
        first_block = block_start(tree_level, LEVELS)
        blocks = anc_blocks[::group_size, first_block:first_block + LEVELS - tree_level].astype(jnp.float32)
        product = jnp.einsum("gkab,gbr->gkar", blocks, z_level.astype(jnp.float32))
        y_list.append(product[:, 0].astype(jnp.bfloat16))
        for above in range(tree_level + 1, LEVELS):
            lowered = lowered.at[::group_size, above].add(product[:, above - tree_level])
    answers = [None] * LEVELS
    for tree_level in reversed(range(LEVELS)):
        group_size = 2 ** (tree_level + 1)
        first_block = block_start(tree_level, LEVELS)
        blocks = anc_blocks[::group_size, first_block:first_block + LEVELS - tree_level].astype(jnp.float32)
        pieces_list = [y_list[tree_level]]
        for above in range(tree_level + 1, LEVELS):
            pieces_list.append(-jnp.repeat(answers[above].astype(jnp.bfloat16), 2 ** (above - tree_level), axis=0))
        stacked_vals = jnp.stack(pieces_list, axis=1).astype(jnp.float32)
        answers[tree_level] = jnp.einsum("gkab,gkar->gbr", blocks, stacked_vals)
    x_anc = jnp.stack([jnp.repeat(answers[tree_level], 2 ** (tree_level + 1), axis=0) for tree_level in range(LEVELS)], axis=1)
    solved_bf = x_anc.astype(jnp.bfloat16).reshape(N_LAYER, LEVELS, N_ROW, ANC_DEV, R)
    solved_bf = solved_bf.transpose(0, 2, 1, 3, 4).reshape(devices, LEVELS * ANC_DEV, R)

    def backward_leaf(operands):
        leaf_one, inverse, coupling_one, pattern_one, solved_one = operands
        masked = masked_of(coupling_one, pattern_one)
        back_terms = jnp.dot(masked, solved_one, preferred_element_type=jnp.float32)
        leaf_vb = (leaf_one.reshape(rows_dev, R) - back_terms).astype(jnp.bfloat16)
        return jnp.einsum("kba,kbr->kar", inverse.astype(jnp.float32), leaf_vb.reshape(SN_DEV, B, R).astype(jnp.float32))

    x_leaf = lax.map(backward_leaf, (leaf_y, inverse_dev, coupling_dev, pattern_dev, solved_bf))
    return x_leaf.reshape(LEAF_ROWS, R), x_anc
```

```python
import jax
import jax.numpy as jnp
from jax import lax
from jax.sharding import PartitionSpec as P


def swap_pairs(value, axis, bit):
    mask = 2**bit
    pairs = [(source, source ^ mask) for source in range(lax.axis_size(axis))]
    return lax.ppermute(value, axis, pairs)


def pair_groups(bit, layers, rows):
    groups = []
    for low in range(layers):
        if low >> bit & 1:
            continue
        groups.append(
            [low * rows + r for r in range(rows)] + [(low ^ (1 << bit)) * rows + r for r in range(rows)]
        )
    return groups


def exchange(payload, bit):
    groups = pair_groups(bit, lax.axis_size("layer"), lax.axis_size("row"))
    return lax.all_to_all(payload, ("layer", "row"), 0, 0, axis_index_groups=groups)


def block_start(tree_level, level_total):
    return tree_level * level_total - tree_level * (tree_level - 1) // 2


def body(leaf_rhs, leaf_inv, coupling, pattern, anc_rhs, anc_blocks):
    levels_here = anc_rhs.shape[1]
    supers = leaf_inv.shape[0]
    block_width = leaf_inv.shape[1]
    num_sides = leaf_rhs.shape[1]
    sep_rows = anc_rhs.shape[2]
    leaf_rows = supers * block_width
    row_count = lax.axis_size("row")
    layer_pos = lax.axis_index("layer")
    leaf_y = jnp.einsum(
        "kab,kbr->kar",
        leaf_inv,
        leaf_rhs.reshape(supers, block_width, num_sides),
        preferred_element_type=jnp.float32,
    )
    leaf_yb = leaf_y.astype(jnp.bfloat16).reshape(leaf_rows, num_sides)
    masked = (
        coupling.reshape(supers, block_width, levels_here, sep_rows)
        * pattern.astype(jnp.bfloat16)[:, None, :, None]
    )
    masked = masked.reshape(leaf_rows, levels_here * sep_rows)
    leaf_terms = lax.dot_general(
        masked, leaf_yb, (((0,), (0,)), ((), ())), preferred_element_type=jnp.float32
    )
    pending = anc_rhs[0] - leaf_terms.reshape(levels_here, sep_rows, num_sides)
    solved = []
    width = num_sides
    for tree_level in range(levels_here):
        first_block = block_start(tree_level, levels_here)
        block_count = levels_here - tree_level
        stacked = anc_blocks[0, first_block : first_block + block_count].reshape(
            block_count * sep_rows, -1
        )
        upper = (layer_pos >> tree_level & 1) == 1
        half = width // 2
        wire = jnp.bfloat16 if tree_level < 2 else jnp.float32
        if block_count > 1:
            low, high = pending[1:, :, :half], pending[1:, :, half:]
            kept = jnp.where(upper, high, low)
            sent = jnp.where(upper, low, high)
            got = swap_pairs(sent.astype(wire), "layer", tree_level)
        mine = pending[0].astype(wire)
        payload = jnp.stack([mine[:, :half], mine[:, half:]])
        payload = jnp.broadcast_to(payload[:, None], (2, row_count, sep_rows, half))
        pieces = exchange(payload.reshape(2 * row_count, sep_rows, half), tree_level)
        pieces = pieces.reshape(2, row_count * sep_rows, half).astype(jnp.float32)
        level_z = (pieces[0] + pieces[1]).astype(jnp.bfloat16)
        product = jnp.dot(stacked, level_z, preferred_element_type=jnp.float32)
        solved.append(product[:sep_rows].astype(jnp.bfloat16))
        if block_count > 1:
            later_terms = product[sep_rows:].reshape(block_count - 1, sep_rows, half)
            pending = kept + got.astype(jnp.float32) - later_terms
        width = half
    answers = None
    for tree_level in reversed(range(levels_here)):
        first_block = block_start(tree_level, levels_here)
        block_count = levels_here - tree_level
        upper = (layer_pos >> tree_level & 1) == 1
        wire = jnp.bfloat16 if tree_level < 2 else jnp.float32
        factor = anc_blocks[0, first_block : first_block + block_count]
        stacked_vals = solved[tree_level][None]
        if answers is not None:
            answers_b = answers.astype(jnp.bfloat16)
            got = swap_pairs(answers_b if wire == jnp.bfloat16 else answers, "layer", tree_level)
            stacked_vals = jnp.concatenate([stacked_vals, -answers_b])
        partial = lax.dot_general(
            factor,
            stacked_vals,
            (((0, 1), (0, 1)), ((), ())),
            preferred_element_type=jnp.float32,
        )
        partial = partial.astype(wire).reshape(1, row_count, sep_rows, width)
        payload = jnp.broadcast_to(partial, (2, row_count, sep_rows, width))
        pieces = exchange(payload.reshape(2 * row_count, sep_rows, width), tree_level)
        pieces = pieces.reshape(2, row_count, sep_rows, width).astype(jnp.float32).sum(axis=1)
        fresh = jnp.concatenate([pieces[0], pieces[1]], axis=-1)[None]
        if answers is not None:
            got = got.astype(jnp.float32)
            low = jnp.where(upper, got, answers)
            high = jnp.where(upper, answers, got)
            fresh = jnp.concatenate([fresh, jnp.concatenate([low, high], axis=-1)])
        answers = fresh
        width = 2 * width
    anc_out = answers
    solved_bf = anc_out.astype(jnp.bfloat16).reshape(levels_here * sep_rows, num_sides)
    back_terms = jnp.dot(masked, solved_bf, preferred_element_type=jnp.float32)
    leaf_vb = (leaf_y.reshape(leaf_rows, num_sides) - back_terms).astype(jnp.bfloat16)
    x_leaf = jnp.einsum(
        "kba,kbr->kar",
        leaf_inv,
        leaf_vb.reshape(supers, block_width, num_sides),
        preferred_element_type=jnp.float32,
    )
    return (x_leaf.reshape(leaf_rows, num_sides), anc_out[None])


def solution(mesh):
    placed = (
        P(("layer", "row"), None),
        P(("layer", "row"), None, None),
        P(("layer", "row"), None, None),
        P(("layer", "row"), None),
        P("layer", None, "row", None),
        P("layer", None, "row", None),
    )
    return jax.shard_map(
        body,
        mesh=mesh,
        in_specs=placed,
        out_specs=(P(("layer", "row"), None), P("layer", None, "row", None)),
        check_vma=False,
    )
```

```python
import functools

import jax
import jax.numpy as jnp
from jax import lax
from jax.experimental import pallas as pl
from jax.experimental.pallas import tpu as pltpu
from jax.sharding import PartitionSpec as P

BF = jnp.bfloat16
F32 = jnp.float32
LEVELS = 5
SEP = 128
COLS = 128
CHIPS = 4
AXES = ("layer", "row")
VMEM = pl.BlockSpec(memory_space=pltpu.VMEM)
SMEM = pl.BlockSpec(memory_space=pltpu.SMEM)
ANY = pl.BlockSpec(memory_space=pl.ANY)
PARAMS = pltpu.CompilerParams(vmem_limit_bytes=40 * 1024 * 1024)


def block_start(level):
    return level * LEVELS - level * (level - 1) // 2


def devices():
    return lax.axis_size("layer") * lax.axis_size("row")


def send_xor(value, mask):
    return lax.ppermute(value, AXES, [(i, i ^ mask) for i in range(devices())])


def send_ring(value, step):
    pairs = [(i, (i & ~6) | ((((i >> 1 & 3) + step) % CHIPS) << 1)) for i in range(devices())]
    return lax.ppermute(value, AXES, pairs)


def lanes(start, size=128):
    return pl.ds(pl.multiple_of(start * size, size), size)


def dot(a, b):
    return jnp.dot(a, b, preferred_element_type=F32)


def leaf_kernel(pos, pattern, rhs, inv, coup, anc, own0, own, *sends):
    share, yb, cm = sends[-3:]
    for k in range(8):
        rows = pl.ds(k * 128, 128)
        yb[rows, :] = dot(inv[k], rhs[rows, :]).astype(BF)
    group = pos[2]
    for t in range(LEVELS):
        for k in range(8):
            rows = pl.ds(k * 128, 128)
            keep = pattern[k, t].astype(F32)
            cm[rows, :] = (coup[t, rows, :].astype(F32) * keep).astype(BF)
        terms = lax.dot_general(cm[...], yb[...], (((0,), (0,)), ((), ())), preferred_element_type=F32)
        share[...] = anc[t] - terms
        piece = share[:, lanes(group)]
        if t == 0:
            own0[...] = piece
        else:
            own[t - 1] = piece
        for m in range(1, 4):
            piece = share[:, lanes(group ^ m)].astype(BF)
            if t == 0:
                sends[m - 1][...] = piece
            else:
                sends[2 + m][t - 1] = piece


def load_blocks(first, count, pos, own_blocks, oth_blocks, blk, sems):
    core = pos[1]
    copies = []
    for k in range(count):
        copies.append(
            (
                pltpu.make_async_copy(own_blocks.at[first + k], blk.at[k, core], sems.at[0, k]),
                pltpu.make_async_copy(oth_blocks.at[first + k], blk.at[k, 1 - core], sems.at[1, k]),
            )
        )
    for pair in copies:
        for one in pair:
            one.start()
    return copies


def forward_kernel(level, pos, own_blocks, oth_blocks, z0, z1, z2, z3, *refs):
    count = LEVELS - level
    first = block_start(level)
    if level == 0:
        own, p1, p2, p3, *refs = refs
    elif count > 1:
        pend, *refs = refs
    if count > 1:
        y_out, pend_out, v_out, blk, zabs, sems = refs
    else:
        y_out, blk, zabs, sems = refs
    copies = load_blocks(first, count, pos, own_blocks, oth_blocks, blk, sems)
    chip, core = pos[0], pos[1]
    for d, z in enumerate((z0, z1, z2, z3)):
        zabs[lanes((chip + CHIPS - d) % CHIPS, 256), :] = z[...]
    if level == 0:
        for k in range(count - 1):
            pend_out[k, lanes(core), :] = own[k] + p2[k].astype(F32)
            pend_out[k, lanes(1 - core), :] = p1[k].astype(F32) + p3[k].astype(F32)
    z = zabs[...]
    for k in range(count):
        for one in copies[k]:
            one.wait()
        product = dot(blk[k].reshape(256, 1024), z)
        if k == 0:
            y_out[...] = product.T.astype(BF)
        else:
            base = pend_out[k - 1] if level == 0 else pend[k]
            after = base - product
            pend_out[k - 1] = after
            if k == 1:
                v_out[...] = after.astype(BF)


def backward_kernel(level, pos, own_blocks, oth_blocks, y, *refs):
    count = LEVELS - level
    first = block_start(level)
    if count > 1:
        held, g1, g2, g3, *refs = refs
        above, refs = refs[: count - 2], refs[count - 2 :]
        sol_out, solb_out, own_out, s1, s2, s3, blk, vals, sems = refs
    else:
        own_out, s1, s2, s3, blk, vals, sems = refs
    copies = load_blocks(first, count, pos, own_blocks, oth_blocks, blk, sems)
    chip = pos[0]
    vals[:, 0:256] = y[...]
    if count > 1:
        sol = held[...] + g1[...].astype(F32) + g2[...].astype(F32) + g3[...].astype(F32)
        sol_out[...] = sol
        solb_out[...] = sol.astype(BF)
        vals[:, 256:512] = (-sol).astype(BF)
        for k in range(2, count):
            vals[:, 256 * k : 256 * (k + 1)] = -above[k - 2][...]
    for pair in copies:
        for one in pair:
            one.wait()
    stack = blk.reshape(count * 256, 1024)
    for d, out in enumerate((own_out, s1, s2, s3)):
        part = dot(vals[...], stack[:, lanes((chip + d) % CHIPS, 256)])
        out[...] = part.astype(out.dtype)


def final_kernel(pos, pattern, rhs, inv, coup, *refs):
    sol0, got0, sol, got, x_leaf, x_anc, solved, cm, back = refs[0], refs[1:4], refs[4:8], refs[8:11], *refs[11:]
    group, core = pos[2], pos[1]
    for t in range(LEVELS):
        mine = sol0 if t == 0 else sol[t - 1]
        x_anc[t, :, lanes(group)] = mine[:, lanes(core)].T
        for m in range(1, 4):
            piece = got0[m - 1][...] if t == 0 else got[m - 1][t - 1]
            x_anc[t, :, lanes(group ^ m)] = piece.astype(F32).T
        solved[...] = x_anc[t].astype(BF)
        for k in range(8):
            rows = pl.ds(k * 128, 128)
            keep = pattern[k, t].astype(F32)
            cm[rows, :] = (coup[t, rows, :].astype(F32) * keep).astype(BF)
        terms = dot(cm[...], solved[...])
        if t == 0:
            back[...] = terms
        else:
            back[...] += terms
    for k in range(8):
        rows = pl.ds(k * 128, 128)
        leaf_vb = (dot(inv[k], rhs[rows, :]) - back[rows, :]).astype(BF)
        x_leaf[rows, :] = lax.dot_general(inv[k], leaf_vb, (((0,), (0,)), ((), ())), preferred_element_type=F32)


def shape(dims, dtype):
    return jax.ShapeDtypeStruct(dims, dtype)


def body(leaf_rhs, leaf_inv, coupling, pattern, anc_rhs, anc_blocks):
    layer, row = lax.axis_index("layer"), lax.axis_index("row")
    chip, core = row // 2, row % 2
    group = (layer % 2) * 2 + core
    pos = jnp.stack([chip, core, group]).astype(jnp.int32)
    coup = coupling.transpose(1, 0, 2)
    own_blocks = anc_blocks[0]

    outs = pl.pallas_call(
        leaf_kernel,
        out_shape=[shape((SEP, COLS), F32), shape((4, SEP, COLS), F32)]
        + [shape((SEP, COLS), BF)] * 3
        + [shape((4, SEP, COLS), BF)] * 3,
        in_specs=[SMEM, SMEM, VMEM, VMEM, VMEM, VMEM],
        out_specs=[VMEM] * 8,
        scratch_shapes=[pltpu.VMEM((SEP, 512), F32), pltpu.VMEM((1024, 512), BF), pltpu.VMEM((1024, 128), BF)],
        compiler_params=PARAMS,
        name="leaf_forward",
    )(pos, pattern, leaf_rhs, leaf_inv, coup, anc_rhs[0])
    own0, own, sends0, sends = outs[0], outs[1], outs[2:5], outs[5:8]
    masks = (1, 8, 9)
    first_got = [send_xor(s, m) for s, m in zip(sends0, masks)]
    oth_blocks = send_xor(own_blocks, 1)
    later_got = [send_xor(s, m) for s, m in zip(sends, masks)]

    near = own0 + first_got[1].astype(F32)
    far = first_got[0].astype(F32) + first_got[2].astype(F32)
    flip = core == 1
    v = jnp.concatenate([jnp.where(flip, far, near), jnp.where(flip, near, far)]).astype(BF)

    ys = []
    pend = None
    for t in range(LEVELS):
        count = LEVELS - t
        zs = [v] + [send_ring(v, d) for d in (1, 2, 3)]
        extra = [own] + later_got if t == 0 else ([pend] if count > 1 else [])
        out_shape = [shape((COLS, 256), BF)]
        if count > 1:
            out_shape += [shape((count - 1, 256, COLS), F32), shape((256, COLS), BF)]
        outs = pl.pallas_call(
            functools.partial(forward_kernel, t),
            out_shape=out_shape,
            in_specs=[SMEM, ANY, ANY] + [VMEM] * (4 + len(extra)),
            out_specs=[VMEM] * len(out_shape),
            scratch_shapes=[
                pltpu.VMEM((count, 2, SEP, 1024), BF),
                pltpu.VMEM((1024, COLS), BF),
                pltpu.SemaphoreType.DMA((2, count)),
            ],
            compiler_params=PARAMS,
            name=f"forward_level{t}",
        )(pos, own_blocks, oth_blocks, *zs, *extra)
        ys.append(outs[0])
        if count > 1:
            pend, v = outs[1], outs[2]
        if t == 3:
            low = jnp.stack(ys[1:])
            a, b, c = send_xor(low, 16), send_xor(low[1:], 32), send_xor(low[1:], 48)
            ys[1] = (ys[1].astype(F32) + a[0].astype(F32)).astype(BF)
            both = low[1:].astype(F32) + a[1:].astype(F32) + b.astype(F32) + c.astype(F32)
            ys[2] = both[0].astype(BF)
            third = both[1].astype(BF)
            ys[3] = (third.astype(F32) + send_xor(third, 64).astype(F32)).astype(BF)
    top = ys[4]
    for bits in ((16, 32, 48), (64, 128, 192)):
        got = [send_xor(top, m).astype(F32) for m in bits]
        top = (top.astype(F32) + got[0] + (got[1] + got[2])).astype(BF)
    ys[4] = top

    sols, solbs = [], []
    pieces = None
    for t in reversed(range(LEVELS)):
        count = LEVELS - t
        args = [ys[t]]
        out_shape = []
        if count > 1:
            args += list(pieces) + solbs[::-1]
            out_shape = [shape((COLS, 256), F32), shape((COLS, 256), BF)]
        out_shape = out_shape + [shape((COLS, 256), F32)] + [shape((COLS, 256), BF)] * 3
        outs = pl.pallas_call(
            functools.partial(backward_kernel, t),
            out_shape=out_shape,
            in_specs=[SMEM, ANY, ANY] + [VMEM] * len(args),
            out_specs=[VMEM] * len(out_shape),
            scratch_shapes=[
                pltpu.VMEM((count, 2, SEP, 1024), BF),
                pltpu.VMEM((COLS, count * 256), BF),
                pltpu.SemaphoreType.DMA((2, count)),
            ],
            compiler_params=PARAMS,
            name=f"backward_level{t}",
        )(pos, own_blocks, oth_blocks, *args)
        if count > 1:
            sols.append(outs[0])
            solbs.append(outs[1])
            outs = outs[2:]
        pieces = [outs[0]] + [send_ring(outs[d], d) for d in (1, 2, 3)]
    sols, solbs = sols[::-1], solbs[::-1]

    def halves(value):
        low, high = value[..., :SEP], value[..., SEP:]
        return jnp.where(flip, high, low), jnp.where(flip, low, high)

    same, other = halves(jnp.stack(solbs))
    got = [send_xor(other, 1), send_xor(same, 8), send_xor(other, 9)]
    sol0 = pieces[0] + pieces[1].astype(F32) + pieces[2].astype(F32) + pieces[3].astype(F32)
    same, other = halves(sol0.astype(BF))
    got0 = [send_xor(other, 1), send_xor(same, 8), send_xor(other, 9)]

    x_leaf, x_anc = pl.pallas_call(
        final_kernel,
        out_shape=[shape((1024, 512), F32), shape((LEVELS, SEP, 512), F32)],
        in_specs=[SMEM, SMEM] + [VMEM] * 14,
        out_specs=[VMEM] * 2,
        scratch_shapes=[pltpu.VMEM((SEP, 512), BF), pltpu.VMEM((1024, 128), BF), pltpu.VMEM((1024, 512), F32)],
        compiler_params=PARAMS,
        name="leaf_backward",
    )(pos, pattern, leaf_rhs, leaf_inv, coup, sol0, *got0, *sols, *got)
    return x_leaf, x_anc[None]


def solution(mesh):
    placed = (
        P(("layer", "row"), None),
        P(("layer", "row"), None, None),
        P(("layer", "row"), None, None),
        P(("layer", "row"), None),
        P("layer", None, "row", None),
        P("layer", None, "row", None),
    )
    return jax.shard_map(
        body,
        mesh=mesh,
        in_specs=placed,
        out_specs=(P(("layer", "row"), None), P("layer", None, "row", None)),
        check_vma=False,
    )
```

```python
import functools

import jax
import jax.numpy as jnp
from jax import lax
from jax.experimental import pallas as pl
from jax.experimental.pallas import tpu as pltpu
from jax.sharding import PartitionSpec as P

BF = jnp.bfloat16
F32 = jnp.float32
LEVELS = 5
SEP = 128
COLS = 128
CHIPS = 4
AXES = ("layer", "row")
VMEM = pl.BlockSpec(memory_space=pltpu.VMEM)
SMEM = pl.BlockSpec(memory_space=pltpu.SMEM)
ANY = pl.BlockSpec(memory_space=pl.ANY)
PARAMS = pltpu.CompilerParams(vmem_limit_bytes=16 * 1024 * 1024)


def block_start(level):
    return level * LEVELS - level * (level - 1) // 2


def devices():
    return lax.axis_size("layer") * lax.axis_size("row")


def send_xor(value, mask):
    return lax.ppermute(value, AXES, [(i, i ^ mask) for i in range(devices())])


def send_ring(value, step):
    pairs = [(i, (i & ~6) | ((((i >> 1 & 3) + step) % CHIPS) << 1)) for i in range(devices())]
    return lax.ppermute(value, AXES, pairs)


def lanes(start, size=128):
    return pl.ds(pl.multiple_of(start * size, size), size)


def dot(a, b):
    return jnp.dot(a, b, preferred_element_type=F32)


def masked_into(cm, coup, pattern, t):
    for k in range(8):
        rows = pl.ds(k * 128, 128)
        keep = pattern[k, t].astype(F32)
        cm[rows, :] = (coup[t, rows, :].astype(F32) * keep).astype(BF)


def leaf_kernel(pos, pattern, rhs, inv, coup, anc, own0, s1, s2, s3, own, side, cross, share, yb, cm):
    for k in range(8):
        rows = pl.ds(k * 128, 128)
        yb[rows, :] = dot(inv[k], rhs[rows, :]).astype(BF)
    group = pos[2]
    for t in range(LEVELS):
        masked_into(cm, coup, pattern, t)
        terms = lax.dot_general(cm[...], yb[...], (((0,), (0,)), ((), ())), preferred_element_type=F32)
        share[...] = anc[t] - terms
        mine = share[:, lanes(group)]
        others = [share[:, lanes(group ^ m)].astype(BF) for m in (1, 2, 3)]
        if t == 0:
            own0[...] = mine
            for out, piece in zip((s1, s2, s3), others):
                out[...] = piece
        else:
            own[t - 1] = mine
            cross[t - 1, 0] = others[0]
            side[t - 1] = others[1]
            cross[t - 1, 1] = others[2]


def rows_of(blocks, first, count):
    return blocks[first : first + count].reshape(count * SEP, 1024)


def fetch(own_blocks, oth_blocks, runs, blk, fulls, sems):
    copies, at = [], 0
    for first, count in runs:
        for side, blocks in enumerate((own_blocks, oth_blocks)):
            source, target = blocks.at[pl.ds(first, count)], blk.at[side, pl.ds(at, count)]
            copies.append(pltpu.make_async_copy(source, target, sems.at[len(copies)]))
        at += count
    for source, target in fulls:
        copies.append(pltpu.make_async_copy(source, target, sems.at[len(copies)]))
    for one in copies:
        one.start()
    return copies


def wait(copies):
    for one in copies:
        one.wait()


def forward_kernel(level, pos, own_blocks, oth_blocks, z0, z1, z2, z3, *refs):
    count = LEVELS - level
    first = block_start(level)
    if level == 0:
        own, got_core, got_layer, y_out, pend_out, v_out, zabs, blk, sems = refs
    else:
        pend, y_out, pend_out, v_out, zabs, blk, sems = refs
    copies = fetch(own_blocks, oth_blocks, [(first, count)], blk, [], sems)
    chip, core = pos[0], pos[1]
    for d, z in enumerate((z0, z1, z2, z3)):
        zabs[lanes((chip + CHIPS - d) % CHIPS, 256), :] = z[...]
    for side, half in enumerate((core, 1 - core)):
        copies[side].wait()
        product = dot(rows_of(blk.at[side], 0, count), zabs[...])
        y_out[:, lanes(half)] = product[:SEP].T.astype(BF)
        for k in range(count - 1):
            if level == 0:
                base = own[k] if side == 0 else got_core[k, 0].astype(F32)
                base = base + got_layer[k, side].astype(F32)
            else:
                base = pend[k + 1, lanes(half), :]
            after = base - product[(k + 1) * SEP : (k + 2) * SEP]
            pend_out[k, lanes(half), :] = after
            if level == 0 and k == 0:
                v_out[lanes(half), :] = after.astype(BF)
            if level == 1 and k < 2:
                v_out[k, lanes(half), :] = after.astype(BF)


def middle_kernel(pos, own_blocks, oth_blocks, full, z0, z1, z2, z3, pend, y2, y3, v_out, zabs, vabs, blk, whole, sems):
    copies = fetch(own_blocks, oth_blocks, [(9, 1), (11, 3)], blk, [(full, whole)], sems)
    chip, core = pos[0], pos[1]
    for d, z in enumerate((z0, z1, z2, z3)):
        place = lanes((chip + CHIPS - d) % CHIPS, 256)
        zabs[place, :] = z[0]
        vabs[place, :] = z[1]
    copies[4].wait()
    vabs[...] = (vabs[...].astype(F32) - dot(whole[...], zabs[...])).astype(BF)
    wait(copies[:4])
    for side, half in enumerate((core, 1 - core)):
        two = dot(rows_of(blk.at[side], 0, 2), zabs[...])
        three = dot(rows_of(blk.at[side], 2, 2), vabs[...])
        y2[:, lanes(half)] = two[:SEP].T.astype(BF)
        y3[:, lanes(half)] = three[:SEP].T.astype(BF)
        after = pend[2, lanes(half), :] - two[SEP:] - three[SEP:]
        v_out[lanes(half), :] = after.astype(BF)


def hand_out(part, level_at, chip, outs):
    for d, out in enumerate(outs):
        out[level_at] = part[:, lanes((chip + d) % CHIPS, 256)].astype(out.dtype)


def top_kernel(pos, own_blocks, oth_blocks, full3, full4, z0, z1, z2, z3, y2, y3, sol_out, solb_out, *refs):
    outs, (zabs, part, blk, whole3, whole4, sems) = refs[:4], refs[4:]
    copies = fetch(own_blocks, oth_blocks, [(9, 1), (11, 3)], blk, [(full4, whole4), (full3, whole3)], sems)
    chip, core = pos[0], pos[1]
    for d, z in enumerate((z0, z1, z2, z3)):
        zabs[lanes((chip + CHIPS - d) % CHIPS, 256), :] = z[...]
    copies[4].wait()
    y4 = dot(whole4[...], zabs[...]).T.astype(BF)
    sol = dot(y4, whole4[:, lanes(chip, 256)])
    sol_out[...] = sol
    solb_out[...] = sol.astype(BF)
    third = second = None
    wait(copies[:4])
    for side, half in enumerate((core, 1 - core)):
        minus = -solb_out[:, lanes(half)]
        one = dot(jnp.concatenate([y3[:, lanes(half)], minus], axis=1), rows_of(blk.at[side], 2, 2))
        two = dot(jnp.concatenate([y2[:, lanes(half)], minus], axis=1), rows_of(blk.at[side], 0, 2))
        third = one if third is None else third + one
        second = two if second is None else second + two
    part[...] = third
    hand_out(part, 1, chip, outs)
    copies[5].wait()
    part[...] = second - dot(third.astype(BF), whole3[...])
    hand_out(part, 0, chip, outs)


def low_kernel(pos, own_blocks, oth_blocks, full1, held, g1, g2, g3, sol4, y0, y1, sol_out, solb_out, *refs):
    outs, (part, vals, blk, whole1, sems) = refs[:4], refs[4:]
    copies = fetch(own_blocks, oth_blocks, [(0, 1), (2, 7)], blk, [(full1, whole1)], sems)
    chip, core = pos[0], pos[1]
    for k in range(2):
        sol = held[k] + g1[k].astype(F32) + g2[k].astype(F32) + g3[k].astype(F32)
        sol_out[k] = sol
        solb_out[k] = sol.astype(BF)
    solb_out[2] = sol4[...]
    first = zeroth = None
    wait(copies[:4])
    for side, half in enumerate((core, 1 - core)):
        vals[:, 0:SEP] = y1[:, lanes(half)]
        for k in range(3):
            vals[:, SEP * (k + 1) : SEP * (k + 2)] = -solb_out[k, :, lanes(half)]
        one = dot(vals[...], rows_of(blk.at[side], 4, 4))
        both = jnp.concatenate([y0[:, lanes(half)], vals[:, SEP:]], axis=1)
        two = dot(both, rows_of(blk.at[side], 0, 4))
        first = one if first is None else first + one
        zeroth = two if zeroth is None else zeroth + two
    part[...] = first
    hand_out(part, 1, chip, outs)
    copies[4].wait()
    part[...] = zeroth - dot(first.astype(BF), whole1[...])
    hand_out(part, 0, chip, outs)


def final_kernel(pos, pattern, rhs, inv, coup, sol01, got1, got2, got3, sol23, sol4, layer_b, core_b, x_leaf, x_anc, solved, cm, back):
    group, core = pos[2], pos[1]
    mine = lanes(core)
    for t in range(LEVELS):
        if t < 2:
            own = sol01[t, :, mine]
            others = got1[t], got2[t], got3[t]
        else:
            own = sol23[t - 2, :, mine] if t < 4 else sol4[:, mine]
            others = core_b[t - 2, 0], layer_b[t - 2, :, mine], core_b[t - 2, 1]
        x_anc[t, :, lanes(group)] = own.T
        for m in range(1, 4):
            x_anc[t, :, lanes(group ^ m)] = others[m - 1].astype(F32).T
        solved[...] = x_anc[t].astype(BF)
        masked_into(cm, coup, pattern, t)
        terms = dot(cm[...], solved[...])
        if t == 0:
            back[...] = terms
        else:
            back[...] += terms
    for k in range(8):
        rows = pl.ds(k * 128, 128)
        leaf_vb = (dot(inv[k], rhs[rows, :]) - back[rows, :]).astype(BF)
        x_leaf[rows, :] = lax.dot_general(inv[k], leaf_vb, (((0,), (0,)), ((), ())), preferred_element_type=F32)


def shape(dims, dtype):
    return jax.ShapeDtypeStruct(dims, dtype)


def call(kernel, name, outs, scratch, copies, *args):
    specs = [SMEM if a.dtype == jnp.int32 else ANY if copies and a.shape[-1] == 1024 else VMEM for a in args]
    scratch = [pltpu.VMEM(dims, dtype) for dims, dtype in scratch]
    return pl.pallas_call(
        kernel,
        out_shape=outs,
        in_specs=specs,
        out_specs=[VMEM] * len(outs),
        scratch_shapes=scratch + ([pltpu.SemaphoreType.DMA((copies,))] if copies else []),
        compiler_params=PARAMS,
        name=name,
    )(*args)


def add(*values):
    return functools.reduce(jnp.add, [v.astype(F32) for v in values]).astype(BF)


def ring(value):
    return [value] + [send_ring(value, d) for d in (1, 2, 3)]


def body(leaf_rhs, leaf_inv, coupling, pattern, anc_rhs, anc_blocks):
    layer, row = lax.axis_index("layer"), lax.axis_index("row")
    chip, core = row // 2, row % 2
    group = (layer % 2) * 2 + core
    flip = core == 1
    pos = jnp.stack([chip, core, group]).astype(jnp.int32)
    coup = coupling.transpose(1, 0, 2)
    blocks = anc_blocks[0]

    def whole(k):
        return lax.all_gather(blocks[k], "row", axis=0, tiled=True)

    full3, full4, full1 = whole(10), whole(14), whole(1)

    own0, s1, s2, s3, own, side, cross = call(
        leaf_kernel,
        "leaf_forward",
        [shape((SEP, COLS), F32)]
        + [shape((SEP, COLS), BF)] * 3
        + [shape((4, SEP, COLS), F32), shape((4, SEP, COLS), BF), shape((4, 2, SEP, COLS), BF)],
        [((SEP, 512), F32), ((1024, 512), BF), ((1024, 128), BF)],
        0,
        *(pos, pattern, leaf_rhs, leaf_inv, coup, anc_rhs[0]),
    )
    late_blocks, s1 = lax.optimization_barrier((blocks, s1))
    got = [send_xor(s, m) for s, m in zip((s1, s2, s3), (1, 8, 9))]
    got_core = send_xor(cross, 1)
    oth = send_xor(late_blocks, 1)
    got_layer = send_xor(jnp.stack([side, got_core[:, 1]], axis=1), 8)
    near = own0 + got[1].astype(F32)
    far = got[0].astype(F32) + got[2].astype(F32)
    v = jnp.concatenate([jnp.where(flip, far, near), jnp.where(flip, near, far)]).astype(BF)

    zscratch, wide = ((1024, COLS), BF), ((1024, 1024), BF)
    y0, pend, v = call(
        functools.partial(forward_kernel, 0),
        "forward_level0",
        [shape((COLS, 256), BF), shape((4, 256, COLS), F32), shape((256, COLS), BF)],
        [zscratch, ((2, 5, SEP, 1024), BF)],
        2,
        *(pos, blocks, oth, *ring(v), own, got_core, got_layer),
    )
    y1, pend, v = call(
        functools.partial(forward_kernel, 1),
        "forward_level1",
        [shape((COLS, 256), BF), shape((3, 256, COLS), F32), shape((2, 256, COLS), BF)],
        [zscratch, ((2, 4, SEP, 1024), BF)],
        2,
        *(pos, blocks, oth, *ring(v), pend),
    )
    y2, y3, v = call(
        middle_kernel,
        "forward_levels23",
        [shape((COLS, 256), BF), shape((COLS, 256), BF), shape((256, COLS), BF)],
        [zscratch, zscratch, ((2, 4, SEP, 1024), BF), wide],
        5,
        *(pos, blocks, oth, full3, *ring(v), pend),
    )
    v = add(v, *[send_xor(v, m) for m in (16, 32, 48)])
    v, y1, y2, y3 = lax.optimization_barrier((v, y1, y2, y3))
    z4 = add(v, *[send_xor(v, m) for m in (64, 128, 192)])
    low = jnp.stack([y2, y3])
    low = add(low, *[send_xor(low, m) for m in (16, 32, 48)])
    y3 = add(low[1], send_xor(low[1], 64))
    y2 = low[0]
    y1 = add(y1, send_xor(y1, 16))
    pieces = [shape((2, COLS, 256), F32)] + [shape((2, COLS, 256), BF)] * 3
    sol4, sol4b, *parts = call(
        top_kernel,
        "top_levels",
        [shape((COLS, 256), F32), shape((COLS, 256), BF)] + pieces,
        [zscratch, ((COLS, 1024), F32), ((2, 4, SEP, 1024), BF), wide, wide],
        6,
        *(pos, blocks, oth, full3, full4, *ring(z4), y2, y3),
    )
    parts = [parts[0]] + [send_ring(parts[d], d) for d in (1, 2, 3)]
    sol23, upper, *parts = call(
        low_kernel,
        "low_levels",
        [shape((2, COLS, 256), F32), shape((3, COLS, 256), BF)] + pieces,
        [((COLS, 1024), F32), ((COLS, 4 * SEP), BF), ((2, 8, SEP, 1024), BF), wide],
        5,
        *(pos, blocks, oth, full1, *parts, sol4b, y0, y1),
    )
    parts = [parts[0]] + [send_ring(parts[d], d) for d in (1, 2, 3)]

    def halves(value):
        low, high = value[..., :SEP], value[..., SEP:]
        return jnp.where(flip, high, low), jnp.where(flip, low, high)

    layer_b = send_xor(upper, 8)
    core_b = send_xor(jnp.stack([halves(upper)[1], halves(layer_b)[1]], axis=1), 1)
    sol01 = parts[0] + parts[1].astype(F32) + parts[2].astype(F32) + parts[3].astype(F32)
    same, other = halves(sol01.astype(BF))
    got = [send_xor(other, 1), send_xor(same, 8), send_xor(other, 9)]
    x_leaf, x_anc = call(
        final_kernel,
        "leaf_backward",
        [shape((1024, 512), F32), shape((LEVELS, SEP, 512), F32)],
        [((SEP, 512), BF), ((1024, 128), BF), ((1024, 512), F32)],
        0,
        *(pos, pattern, leaf_rhs, leaf_inv, coup, sol01, *got, sol23, sol4, layer_b, core_b),
    )
    return x_leaf, x_anc[None]


def solution(mesh):
    placed = (
        P(("layer", "row"), None),
        P(("layer", "row"), None, None),
        P(("layer", "row"), None, None),
        P(("layer", "row"), None),
        P("layer", None, "row", None),
        P("layer", None, "row", None),
    )
    return jax.shard_map(
        body,
        mesh=mesh,
        in_specs=placed,
        out_specs=(P(("layer", "row"), None), P("layer", None, "row", None)),
        check_vma=False,
    )
```

```python
import functools

import jax
import jax.numpy as jnp
from jax import lax
from jax.experimental import pallas as pl
from jax.experimental.pallas import tpu as pltpu
from jax.sharding import PartitionSpec as P

BF = jnp.bfloat16
F32 = jnp.float32
LEVELS = 5
SUPERS = 8
SEP = 128
ROWS = 256
ANC = 1024
COLS = 128
QUART = 32
LEAF_MIB = 58
CHIPS = 4
AXES = ("layer", "row")
PLACES = {
    "s": pl.BlockSpec(memory_space=pltpu.SMEM),
    "v": pl.BlockSpec(memory_space=pltpu.VMEM),
    "a": pl.BlockSpec(memory_space=pl.ANY),
}
WHOLE = (10, 14, 1)


def block_start(level):
    return level * LEVELS - level * (level - 1) // 2


def devices():
    return lax.axis_size("layer") * lax.axis_size("row")


def send_xor(value, mask):
    return lax.ppermute(value, AXES, [(i, i ^ mask) for i in range(devices())])


def send_ring(value, step):
    pairs = [(i, (i & ~6) | ((((i >> 1 & 3) + step) % CHIPS) << 1)) for i in range(devices())]
    return lax.ppermute(value, AXES, pairs)


def ring(value):
    return [value] + [send_ring(value, d) for d in (1, 2, 3)]


def part(start, size):
    return pl.ds(pl.multiple_of(start * size, size), size)


def dot(a, b):
    return jnp.dot(a, b, preferred_element_type=F32)


def dot_nt(a, b):
    return lax.dot_general(a, b, (((1,), (1,)), ((), ())), preferred_element_type=F32)


def dot_tn(a, b):
    return lax.dot_general(a, b, (((0,), (0,)), ((), ())), preferred_element_type=F32)


def start(pairs, sems):
    copies = [pltpu.make_async_copy(a, b, sems.at[i]) for i, (a, b) in enumerate(pairs)]
    for one in copies:
        one.start()
    return copies


def wait(copies):
    for one in copies:
        one.wait()


def runs_of(own, oth, runs, blk):
    pairs, at = [], 0
    for first, count in runs:
        for side, blocks in enumerate((own, oth)):
            pairs.append((blocks.at[pl.ds(first, count)], blk.at[side, pl.ds(at, count)]))
        at += count
    return pairs


def whole_of(index, own, oth, around, pos, target):
    chip, core = pos[0], pos[1]
    pairs = []
    for d in range(CHIPS):
        row = 2 * ((chip + CHIPS - d) % CHIPS)
        if d == 0:
            sources = own.at[WHOLE[index]], oth.at[WHOLE[index]]
        else:
            sources = around[d - 1].at[index], around[2 + d].at[index]
        for source, c in zip(sources, (core, 1 - core)):
            pairs.append((source, target.at[part(row + c, SEP)]))
    return pairs


def stack_of(blk, side, first, count):
    return blk[side, first : first + count].reshape(count * SEP, ANC)


def masked_into(cm, coup, pattern, t):
    for k in range(SUPERS):
        rows = pl.ds(k * SEP, SEP)
        keep = pattern[k, t].astype(F32)
        cm[rows, :] = (coup[t, rows, :].astype(F32) * keep).astype(BF)


def leaf_kernel(pos, pattern, *refs):
    rhs_in, inv_in, coup_in, anc_in, own0, s1, s2, s3, own, side, cross = refs[:11]
    share, yb, cm, rhs, inv, coup, anc, sems = refs[11:]
    pairs = [(inv_in, inv), (rhs_in, rhs)]
    for t in range(LEVELS):
        pairs += [(coup_in.at[t], coup.at[t]), (anc_in.at[t], anc.at[t])]
    copies = start(pairs, sems)
    wait(copies[:2])
    for k in range(SUPERS):
        rows = pl.ds(k * SEP, SEP)
        yb[rows, :] = dot(inv[k], rhs[rows, :]).astype(BF)
    group = pos[2]
    for t in range(LEVELS):
        wait(copies[2 + 2 * t : 4 + 2 * t])
        masked_into(cm, coup, pattern, t)
        share[...] = anc[t] - dot_tn(cm[...], yb[...])
        mine = share[:, part(group, COLS)]
        others = [share[:, part(group ^ m, COLS)].astype(BF) for m in (1, 2, 3)]
        if t == 0:
            own0[...] = mine
            for out, piece in zip((s1, s2, s3), others):
                out[...] = piece
        else:
            own[t - 1] = mine
            cross[t - 1, 0] = others[0]
            side[t - 1] = others[1]
            cross[t - 1, 1] = others[2]


def zeroth_kernel(pos, own, oth, z0, z1, z2, z3, held, got_core, got_layer, y_out, pend, v_out, zabs, blk, sems):
    copies = start(runs_of(own, oth, [(0, 5)], blk), sems)
    chip, core = pos[0], pos[1]
    for d, z in enumerate((z0, z1, z2, z3)):
        zabs[part((chip + CHIPS - d) % CHIPS, ROWS), :] = z[...]
    for side, half in enumerate((core, 1 - core)):
        copies[side].wait()
        product = dot(stack_of(blk, side, 0, 5), zabs[...])
        y_out[:, part(half, SEP)] = product[:SEP].T.astype(BF)
        for k in range(4):
            base = held[k] if side == 0 else got_core[k, 0].astype(F32)
            after = base + got_layer[k, side].astype(F32) - product[(k + 1) * SEP : (k + 2) * SEP]
            pend[k, part(half, SEP), :] = after
            if k == 0:
                v_out[part(half, SEP), :] = after.astype(BF)


def first_kernel(pos, own, oth, z0, z1, z2, z3, pend, y_out, mine, s1, s2, s3, zabs, turned, blk, sems):
    copies = start(runs_of(own, oth, [(5, 4)], blk), sems)
    chip, core, quart = pos[0], pos[1], pos[3]
    for d, z in enumerate((z0, z1, z2, z3)):
        zabs[part((chip + CHIPS - d) % CHIPS, ROWS), :] = z[...]
    for side, half in enumerate((core, 1 - core)):
        copies[side].wait()
        product = dot(stack_of(blk, side, 0, 4), zabs[...])
        y_out[:, part(half, SEP)] = product[:SEP].T.astype(BF)
        for k in range(3):
            after = pend[k + 1, part(half, SEP), :] - product[(k + 1) * SEP : (k + 2) * SEP]
            turned[k, :, part(half, SEP)] = after.T
    for m, out in enumerate((mine, s1, s2, s3)):
        for k in range(3):
            out[k] = turned[k, part(quart ^ m, QUART), :].astype(out.dtype)


def middle_kernel(pos, own, oth, *refs):
    around, (z0, z1, z2, z3, pend, y2, vy, v4), refs = refs[:6], refs[6:14], refs[14:]
    za, zb, blk, whole, sems = refs
    pairs = whole_of(0, own, oth, around, pos, whole) + runs_of(own, oth, [(9, 1), (11, 3)], blk)
    copies = start(pairs, sems)
    chip, core = pos[0], pos[1]
    for d, z in enumerate((z0, z1, z2, z3)):
        place = part((chip + CHIPS - d) % CHIPS, ROWS)
        za[:, place] = z[0]
        zb[:, place] = z[1]
    wait(copies[:8])
    zb[...] = (zb[...].astype(F32) - dot_nt(za[...], whole[...])).astype(BF)
    wait(copies[8:])
    for side, half in enumerate((core, 1 - core)):
        two = dot_nt(za[...], stack_of(blk, side, 0, 2))
        three = dot_nt(zb[...], stack_of(blk, side, 2, 2))
        y2[:, part(half, SEP)] = two[:, :SEP].astype(BF)
        vy[1, :, part(half, SEP)] = three[:, :SEP].astype(BF)
        after = (pend[:, part(half, SEP)] - two[:, SEP:] - three[:, SEP:]).astype(BF)
        vy[0, :, part(half, SEP)] = after
        v4[:, part(half, SEP)] = after


def hand_out(total, level_at, chip, outs):
    for d, out in enumerate(outs):
        out[level_at] = total[:, part((chip + d) % CHIPS, ROWS)].astype(out.dtype)


def top_kernel(pos, own, oth, *refs):
    around, (z0, z1, z2, z3, y2, y3, solb), outs, refs = refs[:6], refs[6:13], refs[13:17], refs[17:]
    za, total, blk, whole4, whole3, sems = refs
    pairs = whole_of(1, own, oth, around, pos, whole4) + runs_of(own, oth, [(9, 1), (11, 3)], blk)
    pairs += whole_of(0, own, oth, around, pos, whole3)
    copies = start(pairs, sems)
    chip, core = pos[0], pos[1]
    for d, z in enumerate((z0, z1, z2, z3)):
        za[:, part((chip + CHIPS - d) % CHIPS, ROWS)] = z[...]
    wait(copies[:8])
    y4 = dot_nt(za[...], whole4[...]).astype(BF)
    solb[...] = dot(y4, whole4[:, part(chip, ROWS)]).astype(BF)
    wait(copies[8:12])
    third = second = None
    for side, half in enumerate((core, 1 - core)):
        minus = -solb[:, part(half, SEP)]
        one = dot(jnp.concatenate([y3[:, part(half, SEP)], minus], axis=1), stack_of(blk, side, 2, 2))
        two = dot(jnp.concatenate([y2[:, part(half, SEP)], minus], axis=1), stack_of(blk, side, 0, 2))
        third = one if third is None else third + one
        second = two if second is None else second + two
    total[...] = third
    hand_out(total, 1, chip, outs)
    wait(copies[12:])
    total[...] = second - dot(third.astype(BF), whole3[...])
    hand_out(total, 0, chip, outs)


def low_kernel(pos, own, oth, *refs):
    around, (u0, u1, u2, u3, y0, y1, solb), outs, refs = refs[:6], refs[6:13], refs[13:17], refs[17:]
    total, vals, blk, whole, sems = refs
    pairs = runs_of(own, oth, [(0, 1), (2, 7)], blk) + whole_of(2, own, oth, around, pos, whole)
    copies = start(pairs, sems)
    chip, core, quart = pos[0], pos[1], pos[3]
    for m, piece in enumerate((u0, u1, u2, u3)):
        for k in range(3):
            solb[k, part(quart ^ m, QUART), :] = piece[k]
    wait(copies[:4])
    first = zeroth = None
    for side, half in enumerate((core, 1 - core)):
        vals[:, 0:SEP] = y1[:, part(half, SEP)]
        for k in range(3):
            vals[:, SEP * (k + 1) : SEP * (k + 2)] = -solb[k, :, part(half, SEP)]
        one = dot(vals[...], stack_of(blk, side, 4, 4))
        both = jnp.concatenate([y0[:, part(half, SEP)], vals[:, SEP:]], axis=1)
        two = dot(both, stack_of(blk, side, 0, 4))
        first = one if first is None else first + one
        zeroth = two if zeroth is None else zeroth + two
    total[...] = first
    hand_out(total, 1, chip, outs)
    wait(copies[4:])
    total[...] = zeroth - dot(first.astype(BF), whole[...])
    hand_out(total, 0, chip, outs)


def final_kernel(pos, pattern, rhs, inv, coup, sol01, got1, got2, got3, upper, layer_b, core_b, *refs):
    leaf_out, anc_out, solved, cm, back, x_leaf, x_anc, sems = refs
    group, core = pos[2], pos[1]
    mine = part(core, SEP)
    copies = []

    def put(source, target):
        one = pltpu.make_async_copy(source, target, sems.at[len(copies)])
        one.start()
        copies.append(one)

    for t in (2, 3, 4, 0, 1):
        if t < 2:
            first = sol01[t, :, mine]
            others = got1[t], got2[t], got3[t]
        else:
            first = upper[t - 2, :, mine].astype(F32)
            others = core_b[t - 2, 0], layer_b[t - 2, :, mine], core_b[t - 2, 1]
        x_anc[t, :, part(group, COLS)] = first.T
        for m in range(1, 4):
            x_anc[t, :, part(group ^ m, COLS)] = others[m - 1].astype(F32).T
        put(x_anc.at[t], anc_out.at[t])
        solved[...] = x_anc[t].astype(BF)
        masked_into(cm, coup, pattern, t)
        terms = dot(cm[...], solved[...])
        if t == 2:
            back[...] = terms
        else:
            back[...] += terms
    for k in range(SUPERS):
        rows = pl.ds(k * SEP, SEP)
        leaf_vb = (dot(inv[k], rhs[rows, :]) - back[rows, :]).astype(BF)
        x_leaf[rows, :] = dot_tn(inv[k], leaf_vb)
        put(x_leaf.at[rows], leaf_out.at[rows])
    wait(copies)


def call(kernel, name, places, outs, scratch, sems, *args, mib=32):
    shapes = [jax.ShapeDtypeStruct(dims, dtype) for dims, dtype in outs]
    scratch = [pltpu.VMEM(dims, dtype) for dims, dtype in scratch] + [pltpu.SemaphoreType.DMA((sems,))]
    here, there = places.split(":")
    return pl.pallas_call(
        kernel,
        out_shape=shapes,
        in_specs=[PLACES[p] for p in here],
        out_specs=[PLACES[there]] * len(outs),
        scratch_shapes=scratch,
        compiler_params=pltpu.CompilerParams(vmem_limit_bytes=mib * 1024 * 1024),
        name=name,
    )(*args)


def add(*values):
    return functools.reduce(jnp.add, [v.astype(F32) for v in values])


def body(leaf_rhs, leaf_inv, coupling, pattern, anc_rhs, anc_blocks):
    layer, row = lax.axis_index("layer"), lax.axis_index("row")
    chip, core = row // 2, row % 2
    flip = core == 1
    pos = jnp.stack([chip, core, (layer % 2) * 2 + core, layer // 2 % 4]).astype(jnp.int32)
    coup = coupling.transpose(1, 0, 2)
    own = anc_blocks[0]

    own0, s1, s2, s3, held, side, cross = call(
        leaf_kernel,
        "leaf_forward",
        "ssaaaa:v",
        [((SEP, COLS), F32)]
        + [((SEP, COLS), BF)] * 3
        + [((4, SEP, COLS), F32), ((4, SEP, COLS), BF), ((4, 2, SEP, COLS), BF)],
        [((SEP, 512), F32), ((1024, 512), BF), ((1024, SEP), BF), ((1024, 512), BF), ((SUPERS, SEP, SEP), BF)]
        + [((LEVELS, 1024, SEP), BF), ((LEVELS, SEP, 512), F32)],
        12,
        *(pos, pattern, leaf_rhs, leaf_inv, coup, anc_rhs[0]),
        mib=LEAF_MIB,
    )
    got = [send_xor(s, m) for s, m in zip((s1, s2, s3), (1, 8, 9))]
    later, side = lax.optimization_barrier((own, side))
    oth = send_xor(later, 1)
    right = send_ring(jnp.stack([later[k] for k in WHOLE]), 1)
    got_core = send_xor(cross, 1)
    got_layer = send_xor(jnp.stack([side, got_core[:, 1]], axis=1), 8)
    near, far = add(own0, got[1]), add(got[0], got[2])
    v = jnp.concatenate([jnp.where(flip, far, near), jnp.where(flip, near, far)]).astype(BF)
    v, oth = lax.optimization_barrier((v, oth))

    long = ((ANC, COLS), BF)
    y0, pend, v = call(
        zeroth_kernel,
        "forward_level0",
        "saavvvvvvv:v",
        [((COLS, ROWS), BF), ((4, ROWS, COLS), F32), ((ROWS, COLS), BF)],
        [long, ((2, 5, SEP, ANC), BF)],
        2,
        *(pos, own, oth, *ring(v), held, got_core, got_layer),
    )
    v, right, later = lax.optimization_barrier((v, right, later))
    opposite = send_ring(right, 1)
    left = send_ring(jnp.stack([later[k] for k in WHOLE]), 3)
    y1, mine, *pieces = call(
        first_kernel,
        "forward_level1",
        "saavvvvv:v",
        [((COLS, ROWS), BF), ((3, QUART, ROWS), F32)] + [((3, QUART, ROWS), BF)] * 3,
        [long, ((3, COLS, ROWS), F32), ((2, 4, SEP, ANC), BF)],
        2,
        *(pos, own, oth, *ring(v), pend),
    )
    pend = add(mine, *[send_xor(p, m) for p, m in zip(pieces, (16, 32, 48))])
    v = pend[:2].astype(BF)
    v, y1, left, opposite = lax.optimization_barrier((v, y1, left, opposite))
    around = [right, opposite, left] + [send_xor(a, 1) for a in (right, opposite, left)]
    thin, wide = ((QUART, ANC), BF), ((ANC, ANC), BF)
    y2, vy, v4 = call(
        middle_kernel,
        "forward_levels23",
        "saaaaaaaavvvvv:v",
        [((QUART, ROWS), BF), ((2, QUART, ROWS), BF), ((QUART, ROWS), BF)],
        [thin, thin, ((2, 4, SEP, ANC), BF), wide],
        12,
        *(pos, own, oth, *around, *ring(v), pend[2]),
    )
    got = send_xor(vy, 64)
    z4 = add(v4, got[0], send_xor(v4, 128), send_xor(v4, 192)).astype(BF)
    y3 = add(vy[1], got[1]).astype(BF)
    sol4, *outs = call(
        top_kernel,
        "top_levels",
        "saaaaaaaavvvvvv:v",
        [((QUART, ROWS), BF), ((2, QUART, ROWS), F32)] + [((2, QUART, ROWS), BF)] * 3,
        [thin, ((QUART, ANC), F32), ((2, 4, SEP, ANC), BF), wide, wide],
        20,
        *(pos, own, oth, *around, *ring(z4), y2, y3),
    )
    sol23 = add(outs[0], *[send_ring(outs[d], d) for d in (1, 2, 3)])
    upper = jnp.concatenate([sol23.astype(BF), sol4[None]])
    y1 = add(y1, send_xor(y1, 16)).astype(BF)
    upper, *outs = call(
        low_kernel,
        "low_levels",
        "saaaaaaaavvvvvv:v",
        [((3, COLS, ROWS), BF), ((2, COLS, ROWS), F32)] + [((2, COLS, ROWS), BF)] * 3,
        [((COLS, ANC), F32), ((COLS, 4 * SEP), BF), ((2, 8, SEP, ANC), BF), wide],
        12,
        *(pos, own, oth, *around, upper, *[send_xor(upper, m) for m in (16, 32, 48)], y0, y1),
    )
    sol01 = add(outs[0], *[send_ring(outs[d], d) for d in (1, 2, 3)])

    def halves(value):
        low, high = value[..., :SEP], value[..., SEP:]
        return jnp.where(flip, high, low), jnp.where(flip, low, high)

    layer_b = send_xor(upper, 8)
    core_b = send_xor(jnp.stack([halves(upper)[1], halves(layer_b)[1]], axis=1), 1)
    same, other = halves(sol01.astype(BF))
    got = [send_xor(other, 1), send_xor(same, 8), send_xor(other, 9)]
    x_leaf, x_anc = call(
        final_kernel,
        "leaf_backward",
        "ssvvvvvvvvvv:a",
        [((1024, 512), F32), ((LEVELS, SEP, 512), F32)],
        [((SEP, 512), BF), ((1024, SEP), BF), ((1024, 512), F32), ((1024, 512), F32), ((LEVELS, SEP, 512), F32)],
        13,
        *(pos, pattern, leaf_rhs, leaf_inv, coup, sol01, *got, upper, layer_b, core_b),
    )
    return x_leaf, x_anc[None]


def solution(mesh):
    placed = (
        P(("layer", "row"), None),
        P(("layer", "row"), None, None),
        P(("layer", "row"), None, None),
        P(("layer", "row"), None),
        P("layer", None, "row", None),
        P("layer", None, "row", None),
    )
    return jax.shard_map(
        body,
        mesh=mesh,
        in_specs=placed,
        out_specs=(P(("layer", "row"), None), P("layer", None, "row", None)),
        check_vma=False,
    )
```

```python
import functools

import jax
import jax.numpy as jnp
from jax import lax
from jax.experimental import pallas as pl
from jax.experimental.pallas import tpu as pltpu
from jax.sharding import PartitionSpec as P

BF = jnp.bfloat16
F32 = jnp.float32
LEVELS = 5
SUPERS = 8
SEP = 128
ROWS = 256
ANC = 1024
COLS = 128
QUART = 32
MIB = 52
LEAF_MIB = 58
CHIPS = 4
AXES = ("layer", "row")
PLACES = {
    "s": pl.BlockSpec(memory_space=pltpu.SMEM),
    "v": pl.BlockSpec(memory_space=pltpu.VMEM),
    "a": pl.BlockSpec(memory_space=pl.ANY),
}
WHOLE = (10, 14, 1)


def block_start(level):
    return level * LEVELS - level * (level - 1) // 2


def devices():
    return lax.axis_size("layer") * lax.axis_size("row")


def send_xor(value, mask):
    return lax.ppermute(value, AXES, [(i, i ^ mask) for i in range(devices())])


def send_ring(value, step):
    pairs = [(i, (i & ~6) | ((((i >> 1 & 3) + step) % CHIPS) << 1)) for i in range(devices())]
    return lax.ppermute(value, AXES, pairs)


def ring(value):
    return [value] + [send_ring(value, d) for d in (1, 2, 3)]


def part(start, size):
    return pl.ds(pl.multiple_of(start * size, size), size)


def dot(a, b):
    return jnp.dot(a, b, preferred_element_type=F32)


def dot_nt(a, b):
    return lax.dot_general(a, b, (((1,), (1,)), ((), ())), preferred_element_type=F32)


def dot_tn(a, b):
    return lax.dot_general(a, b, (((0,), (0,)), ((), ())), preferred_element_type=F32)


def start(pairs, sems):
    copies = [pltpu.make_async_copy(a, b, sems.at[i]) for i, (a, b) in enumerate(pairs)]
    for one in copies:
        one.start()
    return copies


def wait(copies):
    for one in copies:
        one.wait()


def runs_of(own, oth, runs, blk):
    pairs, at = [], 0
    for first, count in runs:
        for side, blocks in enumerate((own, oth)):
            pairs.append((blocks.at[pl.ds(first, count)], blk.at[side, pl.ds(at, count)]))
        at += count
    return pairs


def whole_of(index, own, oth, around, pos, target):
    chip, core = pos[0], pos[1]
    pairs = []
    for side, c in enumerate((core, 1 - core)):
        right, left, low, high = around[4 * side : 4 * side + 4]
        near = (own, oth)[side].at[WHOLE[index]]
        for source, d in ((near, 0), (right.at[index], 1), (left.at[index], 3)):
            row = 2 * ((chip + CHIPS - d) % CHIPS) + c
            pairs.append((source, target.at[part(row, SEP)]))
        row = 2 * (2 * ((chip + 2) % CHIPS) + c)
        pairs.append((low.at[index], target.at[part(row, SEP // 2)]))
        pairs.append((high.at[index], target.at[part(row + 1, SEP // 2)]))
    return pairs


def stack_of(blk, side, first, count):
    return blk[side, first : first + count].reshape(count * SEP, ANC)


def masked_into(cm, coup, pattern, t):
    for k in range(SUPERS):
        rows = pl.ds(k * SEP, SEP)
        keep = pattern[k, t].astype(F32)
        cm[rows, :] = (coup[t, rows, :].astype(F32) * keep).astype(BF)


def leaf_kernel(pos, pattern, *refs):
    rhs_in, inv_in, coup_in, anc_in, keep0, send0, keep, send = refs[:8]
    share, yb, cm, rhs, inv, coup, anc, sems = refs[8:]
    pairs = [(inv_in, inv), (rhs_in, rhs)]
    for t in range(LEVELS):
        pairs += [(coup_in.at[t], coup.at[t]), (anc_in.at[t], anc.at[t])]
    copies = start(pairs, sems)
    wait(copies[:2])
    for k in range(SUPERS):
        rows = pl.ds(k * SEP, SEP)
        yb[rows, :] = dot(inv[k], rhs[rows, :]).astype(BF)
    group = pos[2]
    for t in range(LEVELS):
        wait(copies[2 + 2 * t : 4 + 2 * t])
        masked_into(cm, coup, pattern, t)
        share[...] = anc[t] - dot_tn(cm[...], yb[...])
        for m in range(2):
            mine = share[:, part(group ^ m, COLS)]
            other = share[:, part(group ^ (2 + m), COLS)].astype(BF)
            if t == 0:
                keep0[m], send0[m] = mine, other
            else:
                keep[t - 1, m], send[t - 1, m] = mine, other


def zeroth_kernel(pos, own, oth, z0, z1, z2, z3, keep, got_layer, got_core, y_out, pend, v_out, zabs, blk, sems):
    copies = start(runs_of(own, oth, [(0, 5)], blk), sems)
    chip, core = pos[0], pos[1]
    for d, z in enumerate((z0, z1, z2, z3)):
        zabs[part((chip + CHIPS - d) % CHIPS, ROWS), :] = z[...]
    for side, half in enumerate((core, 1 - core)):
        copies[side].wait()
        product = dot(stack_of(blk, side, 0, 5), zabs[...])
        y_out[:, part(half, SEP)] = product[:SEP].T.astype(BF)
        for k in range(4):
            if side == 0:
                base = keep[k, 0] + got_layer[k, 0].astype(F32)
            else:
                base = got_core[k].astype(F32)
            after = base - product[(k + 1) * SEP : (k + 2) * SEP]
            pend[k, part(half, SEP), :] = after
            if k == 0:
                v_out[part(half, SEP), :] = after.astype(BF)


def first_kernel(pos, own, oth, z0, z1, z2, z3, pend, y_out, mine, s1, s2, s3, zabs, turned, blk, sems):
    copies = start(runs_of(own, oth, [(5, 4)], blk), sems)
    chip, core, quart = pos[0], pos[1], pos[3]
    for d, z in enumerate((z0, z1, z2, z3)):
        zabs[part((chip + CHIPS - d) % CHIPS, ROWS), :] = z[...]
    for side, half in enumerate((core, 1 - core)):
        copies[side].wait()
        product = dot(stack_of(blk, side, 0, 4), zabs[...])
        y_out[:, part(half, SEP)] = product[:SEP].T.astype(BF)
        for k in range(3):
            after = pend[k + 1, part(half, SEP), :] - product[(k + 1) * SEP : (k + 2) * SEP]
            turned[k, :, part(half, SEP)] = after.T
    for m, out in enumerate((mine, s1, s2, s3)):
        for k in range(3):
            out[k] = turned[k, part(quart ^ m, QUART), :].astype(out.dtype)


def middle_kernel(pos, own, oth, *refs):
    around, (z0, z1, z2, z3, pend, y2, vy, v4), refs = refs[:8], refs[8:16], refs[16:]
    za, zb, blk, whole, sems = refs
    pairs = whole_of(0, own, oth, around, pos, whole) + runs_of(own, oth, [(9, 1), (11, 3)], blk)
    copies = start(pairs, sems)
    chip, core = pos[0], pos[1]
    for d, z in enumerate((z0, z1, z2, z3)):
        place = part((chip + CHIPS - d) % CHIPS, ROWS)
        za[:, place] = z[0]
        zb[:, place] = z[1]
    wait(copies[:10])
    zb[...] = (zb[...].astype(F32) - dot_nt(za[...], whole[...])).astype(BF)
    wait(copies[10:])
    for side, half in enumerate((core, 1 - core)):
        two = dot_nt(za[...], stack_of(blk, side, 0, 2))
        three = dot_nt(zb[...], stack_of(blk, side, 2, 2))
        y2[:, part(half, SEP)] = two[:, :SEP].astype(BF)
        vy[1, :, part(half, SEP)] = three[:, :SEP].astype(BF)
        after = (pend[:, part(half, SEP)] - two[:, SEP:] - three[:, SEP:]).astype(BF)
        vy[0, :, part(half, SEP)] = after
        v4[:, part(half, SEP)] = after


def hand_out(total, level_at, chip, outs):
    for d, out in enumerate(outs):
        out[level_at] = total[:, part((chip + d) % CHIPS, ROWS)].astype(out.dtype)


def top_kernel(pos, own, oth, *refs):
    around, (z0, z1, z2, z3, y2, y3, solb), outs, refs = refs[:8], refs[8:15], refs[15:19], refs[19:]
    za, total, blk, whole4, whole3, sems = refs
    pairs = whole_of(1, own, oth, around, pos, whole4) + runs_of(own, oth, [(9, 1), (11, 3)], blk)
    pairs += whole_of(0, own, oth, around, pos, whole3)
    copies = start(pairs, sems)
    chip, core = pos[0], pos[1]
    for d, z in enumerate((z0, z1, z2, z3)):
        za[:, part((chip + CHIPS - d) % CHIPS, ROWS)] = z[...]
    wait(copies[:10])
    y4 = dot_nt(za[...], whole4[...]).astype(BF)
    solb[...] = dot(y4, whole4[:, part(chip, ROWS)]).astype(BF)
    wait(copies[10:14])
    third = second = None
    for side, half in enumerate((core, 1 - core)):
        minus = -solb[:, part(half, SEP)]
        one = dot(jnp.concatenate([y3[:, part(half, SEP)], minus], axis=1), stack_of(blk, side, 2, 2))
        two = dot(jnp.concatenate([y2[:, part(half, SEP)], minus], axis=1), stack_of(blk, side, 0, 2))
        third = one if third is None else third + one
        second = two if second is None else second + two
    total[...] = third
    hand_out(total, 1, chip, outs)
    wait(copies[14:])
    total[...] = second - dot(third.astype(BF), whole3[...])
    hand_out(total, 0, chip, outs)


def low_kernel(pos, own, oth, *refs):
    around, (u0, u1, u2, u3, y0, y1, same, other), outs, refs = refs[:8], refs[8:16], refs[16:20], refs[20:]
    solb, total, vals, blk, whole, sems = refs
    pairs = runs_of(own, oth, [(0, 1), (2, 7)], blk) + whole_of(2, own, oth, around, pos, whole)
    copies = start(pairs, sems)
    chip, core, quart = pos[0], pos[1], pos[3]
    for m, piece in enumerate((u0, u1, u2, u3)):
        for k in range(3):
            solb[k, part(quart ^ m, QUART), :] = piece[k]
    same[...] = solb[:, :, part(core, SEP)]
    other[...] = solb[:, :, part(1 - core, SEP)]
    wait(copies[:4])
    first = zeroth = None
    for side, half in enumerate((core, 1 - core)):
        vals[:, 0:SEP] = y1[:, part(half, SEP)]
        for k in range(3):
            vals[:, SEP * (k + 1) : SEP * (k + 2)] = -solb[k, :, part(half, SEP)]
        one = dot(vals[...], stack_of(blk, side, 4, 4))
        both = jnp.concatenate([y0[:, part(half, SEP)], vals[:, SEP:]], axis=1)
        two = dot(both, stack_of(blk, side, 0, 4))
        first = one if first is None else first + one
        zeroth = two if zeroth is None else zeroth + two
    total[...] = first
    hand_out(total, 1, chip, outs)
    wait(copies[4:])
    total[...] = zeroth - dot(first.astype(BF), whole[...])
    hand_out(total, 0, chip, outs)


def final_kernel(pos, pattern, rhs, inv, coup, sol01, got1, got2, got3, upper, up1, up2, up3, *refs):
    leaf_out, anc_out, solved, cm, back, x_leaf, x_anc, sems = refs
    group, core = pos[2], pos[1]
    mine = part(core, SEP)
    copies = []

    def put(source, target):
        one = pltpu.make_async_copy(source, target, sems.at[len(copies)])
        one.start()
        copies.append(one)

    for t in (2, 3, 4, 0, 1):
        if t < 2:
            first = sol01[t, :, mine]
            others = got1[t], got2[t], got3[t]
        else:
            first = upper[t - 2].astype(F32)
            others = up1[t - 2], up2[t - 2], up3[t - 2]
        x_anc[t, :, part(group, COLS)] = first.T
        for m in range(1, 4):
            x_anc[t, :, part(group ^ m, COLS)] = others[m - 1].astype(F32).T
        put(x_anc.at[t], anc_out.at[t])
        solved[...] = x_anc[t].astype(BF)
        masked_into(cm, coup, pattern, t)
        terms = dot(cm[...], solved[...])
        if t == 2:
            back[...] = terms
        else:
            back[...] += terms
    for k in range(SUPERS):
        rows = pl.ds(k * SEP, SEP)
        leaf_vb = (dot(inv[k], rhs[rows, :]) - back[rows, :]).astype(BF)
        x_leaf[rows, :] = dot_tn(inv[k], leaf_vb)
        put(x_leaf.at[rows], leaf_out.at[rows])
    wait(copies)


def call(kernel, name, places, outs, scratch, sems, *args, mib=MIB, cost=None):
    shapes = [jax.ShapeDtypeStruct(dims, dtype) for dims, dtype in outs]
    scratch = [pltpu.VMEM(dims, dtype) for dims, dtype in scratch] + [pltpu.SemaphoreType.DMA((sems,))]
    here, there = places.split(":")
    return pl.pallas_call(
        kernel,
        out_shape=shapes,
        in_specs=[PLACES[p] for p in here],
        out_specs=[PLACES[there]] * len(outs),
        scratch_shapes=scratch,
        compiler_params=pltpu.CompilerParams(vmem_limit_bytes=mib * 1024 * 1024),
        cost_estimate=cost,
        name=name,
    )(*args)


def add(*values):
    return functools.reduce(jnp.add, [v.astype(F32) for v in values])


def body(leaf_rhs, leaf_inv, coupling, pattern, anc_rhs, anc_blocks):
    layer, row = lax.axis_index("layer"), lax.axis_index("row")
    chip, core = row // 2, row % 2
    flip = core == 1
    pos = jnp.stack([chip, core, (layer % 2) * 2 + core, layer // 2 % 4]).astype(jnp.int32)
    coup = coupling.transpose(1, 0, 2)
    own = anc_blocks[0]

    chosen = jnp.stack([own[k] for k in WHOLE])
    pos, chosen = lax.optimization_barrier((pos, chosen))
    oth = send_xor(own, 1)
    right, left = send_ring(chosen, 1), send_ring(chosen, 3)

    keep0, send0, keep, send = call(
        leaf_kernel,
        "leaf_forward",
        "ssaaaa:v",
        [((2, SEP, COLS), F32), ((2, SEP, COLS), BF), ((4, 2, SEP, COLS), F32), ((4, 2, SEP, COLS), BF)],
        [((SEP, 512), F32), ((1024, 512), BF), ((1024, SEP), BF), ((1024, 512), BF), ((SUPERS, SEP, SEP), BF)]
        + [((LEVELS, 1024, SEP), BF), ((LEVELS, SEP, 512), F32)],
        12,
        *(pos, pattern, leaf_rhs, leaf_inv, coup, anc_rhs[0]),
        mib=LEAF_MIB,
        cost=pl.CostEstimate(flops=1, bytes_accessed=1, transcendentals=0),
    )
    got0 = send_xor(send0, 8)
    got0, send = lax.optimization_barrier((got0, send))
    near = add(keep0[0], got0[0])
    far = send_xor(add(keep0[1], got0[1]).astype(BF), 1).astype(F32)
    got_layer = send_xor(send, 8)
    got_core = send_xor(add(keep[:, 1], got_layer[:, 1]).astype(BF), 1)
    v = jnp.concatenate([jnp.where(flip, far, near), jnp.where(flip, near, far)]).astype(BF)
    v, oth, right, left = lax.optimization_barrier((v, oth, right, left))

    long = ((ANC, COLS), BF)
    y0, pend, v = call(
        zeroth_kernel,
        "forward_level0",
        "saavvvvvvv:v",
        [((COLS, ROWS), BF), ((4, ROWS, COLS), F32), ((ROWS, COLS), BF)],
        [long, ((2, 5, SEP, ANC), BF)],
        2,
        *(pos, own, oth, *ring(v), keep, got_layer, got_core),
    )
    v, right, left = lax.optimization_barrier((v, right, left))
    swapped = [send_xor(right, 1), send_xor(left, 1)]
    y1, mine, *pieces = call(
        first_kernel,
        "forward_level1",
        "saavvvvv:v",
        [((COLS, ROWS), BF), ((3, QUART, ROWS), F32)] + [((3, QUART, ROWS), BF)] * 3,
        [long, ((3, COLS, ROWS), F32), ((2, 4, SEP, ANC), BF)],
        2,
        *(pos, own, oth, *ring(v), pend),
    )
    middle = SEP // 2
    pieces, low, high, right, left, swapped = lax.optimization_barrier(
        (pieces, right[:, :middle], left[:, middle:], right, left, swapped)
    )
    low, high = send_ring(low, 1), send_ring(high, 3)
    pend = add(mine, *[send_xor(p, m) for p, m in zip(pieces, (16, 32, 48))])
    v = pend[:2].astype(BF)
    v, y1, low, high = lax.optimization_barrier((v, y1, low, high))
    around = [right, left, low, high] + swapped + [send_xor(low, 1), send_xor(high, 1)]
    thin, wide = ((QUART, ANC), BF), ((ANC, ANC), BF)
    y2, vy, v4 = call(
        middle_kernel,
        "forward_levels23",
        "s" + "a" * 10 + "v" * 5 + ":v",
        [((QUART, ROWS), BF), ((2, QUART, ROWS), BF), ((QUART, ROWS), BF)],
        [thin, thin, ((2, 4, SEP, ANC), BF), wide],
        14,
        *(pos, own, oth, *around, *ring(v), pend[2]),
    )
    got = send_xor(vy, 64)
    z4 = add(v4, got[0], send_xor(v4, 128), send_xor(v4, 192)).astype(BF)
    y3 = add(vy[1], got[1]).astype(BF)
    sol4, *outs = call(
        top_kernel,
        "top_levels",
        "s" + "a" * 10 + "v" * 6 + ":v",
        [((QUART, ROWS), BF), ((2, QUART, ROWS), F32)] + [((2, QUART, ROWS), BF)] * 3,
        [thin, ((QUART, ANC), F32), ((2, 4, SEP, ANC), BF), wide, wide],
        24,
        *(pos, own, oth, *around, *ring(z4), y2, y3),
    )
    sol23 = add(outs[0], *[send_ring(outs[d], d) for d in (1, 2, 3)])
    upper = jnp.concatenate([sol23.astype(BF), sol4[None]])
    y1 = add(y1, send_xor(y1, 16)).astype(BF)
    same, other, *outs = call(
        low_kernel,
        "low_levels",
        "s" + "a" * 10 + "v" * 6 + ":v",
        [((3, COLS, SEP), BF)] * 2 + [((2, COLS, ROWS), F32)] + [((2, COLS, ROWS), BF)] * 3,
        [((3, COLS, ROWS), BF), ((COLS, ANC), F32), ((COLS, 4 * SEP), BF), ((2, 8, SEP, ANC), BF), wide],
        14,
        *(pos, own, oth, *around, upper, *[send_xor(upper, m) for m in (16, 32, 48)], y0, y1),
    )
    sol01 = add(outs[0], *[send_ring(outs[d], d) for d in (1, 2, 3)])
    ups = [send_xor(other, 1), send_xor(same, 8), send_xor(other, 9)]
    sol01, *ups = lax.optimization_barrier((sol01, *ups))
    lower, higher = sol01[..., :SEP].astype(BF), sol01[..., SEP:].astype(BF)
    home, away = jnp.where(flip, higher, lower), jnp.where(flip, lower, higher)
    got = [send_xor(away, 1), send_xor(home, 8), send_xor(away, 9)]
    x_leaf, x_anc = call(
        final_kernel,
        "leaf_backward",
        "ssvvvvvvvvvvv:a",
        [((1024, 512), F32), ((LEVELS, SEP, 512), F32)],
        [((SEP, 512), BF), ((1024, SEP), BF), ((1024, 512), F32), ((1024, 512), F32), ((LEVELS, SEP, 512), F32)],
        13,
        *(pos, pattern, leaf_rhs, leaf_inv, coup, sol01, *got, same, *ups),
    )
    return x_leaf, x_anc[None]


def solution(mesh):
    placed = (
        P(("layer", "row"), None),
        P(("layer", "row"), None, None),
        P(("layer", "row"), None, None),
        P(("layer", "row"), None),
        P("layer", None, "row", None),
        P("layer", None, "row", None),
    )
    return jax.shard_map(
        body,
        mesh=mesh,
        in_specs=placed,
        out_specs=(P(("layer", "row"), None), P("layer", None, "row", None)),
        check_vma=False,
    )
```

```python
import functools

import jax
import jax.numpy as jnp
from jax import lax
from jax.experimental import pallas as pl
from jax.experimental.pallas import tpu as pltpu
from jax.sharding import PartitionSpec as P

BF = jnp.bfloat16
F32 = jnp.float32
LEVELS = 5
SUPERS = 8
SEP = 128
ROWS = 256
ANC = 1024
COLS = 128
QUART = 32
MIB = 52
UPPER_MIB = 58
LEAF_MIB = 58
CHIPS = 4
AXES = ("layer", "row")
PLACES = {
    "s": pl.BlockSpec(memory_space=pltpu.SMEM),
    "v": pl.BlockSpec(memory_space=pltpu.VMEM),
    "a": pl.BlockSpec(memory_space=pl.ANY),
}
WHOLE = (10, 14, 1)


def block_start(level):
    return level * LEVELS - level * (level - 1) // 2


def devices():
    return lax.axis_size("layer") * lax.axis_size("row")


def send_xor(value, mask):
    return lax.ppermute(value, AXES, [(i, i ^ mask) for i in range(devices())])


def send_ring(value, step):
    pairs = [(i, (i & ~6) | ((((i >> 1 & 3) + step) % CHIPS) << 1)) for i in range(devices())]
    return lax.ppermute(value, AXES, pairs)


def ring(value):
    got = {d: send_ring(value, d) for d in (1, 3, 2)}
    return [value] + [got[d] for d in (1, 2, 3)]


def part(start, size):
    return pl.ds(pl.multiple_of(start * size, size), size)


def dot(a, b):
    return jnp.dot(a, b, preferred_element_type=F32)


def dot_nt(a, b):
    return lax.dot_general(a, b, (((1,), (1,)), ((), ())), preferred_element_type=F32)


def dot_tn(a, b):
    return lax.dot_general(a, b, (((0,), (0,)), ((), ())), preferred_element_type=F32)


def start(pairs, sems):
    copies = [pltpu.make_async_copy(a, b, sems.at[i]) for i, (a, b) in enumerate(pairs)]
    for one in copies:
        one.start()
    return copies


def wait(copies):
    for one in copies:
        one.wait()


def runs_of(own, oth, runs, blk):
    pairs, at = [], 0
    for first, count in runs:
        for side, blocks in enumerate((own, oth)):
            pairs.append((blocks.at[pl.ds(first, count)], blk.at[side, pl.ds(at, count)]))
        at += count
    return pairs


def whole_of(index, own, oth, around, pos, target):
    chip, core = pos[0], pos[1]
    pairs = []
    for side, c in enumerate((core, 1 - core)):
        right, left, low, high = around[4 * side : 4 * side + 4]
        near = (own, oth)[side].at[WHOLE[index]]
        for source, d in ((near, 0), (right.at[index], 1), (left.at[index], 3)):
            row = 2 * ((chip + CHIPS - d) % CHIPS) + c
            pairs.append((source, target.at[part(row, SEP)]))
        row = 2 * (2 * ((chip + 2) % CHIPS) + c)
        pairs.append((low.at[index], target.at[part(row, SEP // 2)]))
        pairs.append((high.at[index], target.at[part(row + 1, SEP // 2)]))
    return pairs


def stack_of(blk, side, first, count):
    return blk[side, first : first + count].reshape(count * SEP, ANC)


def masked_into(cm, coup, pattern, t):
    for k in range(SUPERS):
        rows = pl.ds(k * SEP, SEP)
        keep = pattern[k, t].astype(F32)
        cm[rows, :] = (coup[t, rows, :].astype(F32) * keep).astype(BF)


def split_share(share, group, keep, send):
    for m in range(2):
        keep[m] = share[:, part(group ^ m, COLS)]
        send[m] = share[:, part(group ^ (2 + m), COLS)].astype(BF)


def leaf_kernel(pos, pattern, rhs_in, inv_in, coup_in, anc_in, keep, send, yb, share, cm, rhs, inv, coup, anc, sems):
    pairs = [(inv_in, inv), (rhs_in, rhs), (coup_in.at[pl.ds(0, 1)], coup), (anc_in.at[0], anc)]
    copies = start(pairs, sems)
    wait(copies[:2])
    for k in range(SUPERS):
        rows = pl.ds(k * SEP, SEP)
        yb[rows, :] = dot(inv[k], rhs[rows, :]).astype(BF)
    wait(copies[2:])
    masked_into(cm, coup, pattern, 0)
    share[...] = anc[...] - dot_tn(cm[...], yb[...])
    split_share(share, pos[2], keep, send)


def upper_kernel(pos, pattern, coup_in, anc_in, yb, keep, send, share, cm, coup, anc, sems):
    pairs = []
    for t in range(1, LEVELS):
        pairs += [(coup_in.at[t], coup.at[t]), (anc_in.at[t], anc.at[t])]
    copies = start(pairs, sems)
    for t in range(1, LEVELS):
        wait(copies[2 * t - 2 : 2 * t])
        masked_into(cm, coup, pattern, t)
        share[...] = anc[t] - dot_tn(cm[...], yb[...])
        split_share(share, pos[2], keep.at[t - 1], send.at[t - 1])


def zeroth_kernel(pos, own, oth, z0, z1, z2, z3, keep, got_layer, got_core, y_out, pend, v_out, zabs, blk, sems):
    copies = start(runs_of(own, oth, [(0, 5)], blk), sems)
    chip, core = pos[0], pos[1]
    for d, z in enumerate((z0, z1, z2, z3)):
        zabs[part((chip + CHIPS - d) % CHIPS, ROWS), :] = z[...]
    for side, half in enumerate((core, 1 - core)):
        copies[side].wait()
        product = dot(stack_of(blk, side, 0, 5), zabs[...])
        y_out[:, part(half, SEP)] = product[:SEP].T.astype(BF)
        for k in range(4):
            if side == 0:
                base = keep[k, 0] + got_layer[k, 0].astype(F32)
            else:
                base = got_core[k].astype(F32)
            after = base - product[(k + 1) * SEP : (k + 2) * SEP]
            pend[k, part(half, SEP), :] = after
            if k == 0:
                v_out[part(half, SEP), :] = after.astype(BF)


def first_kernel(pos, own, oth, z0, z1, z2, z3, pend, y_out, mine, s1, s2, s3, zabs, turned, blk, sems):
    copies = start(runs_of(own, oth, [(5, 4)], blk), sems)
    chip, core, quart = pos[0], pos[1], pos[3]
    for d, z in enumerate((z0, z1, z2, z3)):
        zabs[part((chip + CHIPS - d) % CHIPS, ROWS), :] = z[...]
    for side, half in enumerate((core, 1 - core)):
        copies[side].wait()
        product = dot(stack_of(blk, side, 0, 4), zabs[...])
        y_out[:, part(half, SEP)] = product[:SEP].T.astype(BF)
        for k in range(3):
            after = pend[k + 1, part(half, SEP), :] - product[(k + 1) * SEP : (k + 2) * SEP]
            turned[k, :, part(half, SEP)] = after.T
    for m, out in enumerate((mine, s1, s2, s3)):
        for k in range(3):
            out[k] = turned[k, part(quart ^ m, QUART), :].astype(out.dtype)


def middle_kernel(pos, own, oth, *refs):
    around, (z0, z1, z2, z3, pend, y2, vy, v4), refs = refs[:8], refs[8:16], refs[16:]
    za, zb, blk, whole, sems = refs
    pairs = whole_of(0, own, oth, around, pos, whole) + runs_of(own, oth, [(9, 1), (11, 3)], blk)
    copies = start(pairs, sems)
    chip, core = pos[0], pos[1]
    for d, z in enumerate((z0, z1, z2, z3)):
        place = part((chip + CHIPS - d) % CHIPS, ROWS)
        za[:, place] = z[0]
        zb[:, place] = z[1]
    wait(copies[:10])
    zb[...] = (zb[...].astype(F32) - dot_nt(za[...], whole[...])).astype(BF)
    wait(copies[10:])
    for side, half in enumerate((core, 1 - core)):
        two = dot_nt(za[...], stack_of(blk, side, 0, 2))
        three = dot_nt(zb[...], stack_of(blk, side, 2, 2))
        y2[:, part(half, SEP)] = two[:, :SEP].astype(BF)
        vy[1, :, part(half, SEP)] = three[:, :SEP].astype(BF)
        after = (pend[:, part(half, SEP)] - two[:, SEP:] - three[:, SEP:]).astype(BF)
        vy[0, :, part(half, SEP)] = after
        v4[:, part(half, SEP)] = after


def hand_out(total, level_at, chip, outs):
    for d, out in enumerate(outs):
        out[level_at] = total[:, part((chip + d) % CHIPS, ROWS)].astype(out.dtype)


def top_kernel(pos, own, oth, *refs):
    around, (z0, z1, z2, z3, y2, y3, solb), outs, refs = refs[:8], refs[8:15], refs[15:19], refs[19:]
    za, total, blk, whole4, whole3, sems = refs
    pairs = whole_of(1, own, oth, around, pos, whole4) + runs_of(own, oth, [(9, 1), (11, 3)], blk)
    pairs += whole_of(0, own, oth, around, pos, whole3)
    copies = start(pairs, sems)
    chip, core = pos[0], pos[1]
    for d, z in enumerate((z0, z1, z2, z3)):
        za[:, part((chip + CHIPS - d) % CHIPS, ROWS)] = z[...]
    wait(copies[:10])
    y4 = dot_nt(za[...], whole4[...]).astype(BF)
    solb[...] = dot(y4, whole4[:, part(chip, ROWS)]).astype(BF)
    wait(copies[10:14])
    third = second = None
    for side, half in enumerate((core, 1 - core)):
        minus = -solb[:, part(half, SEP)]
        one = dot(jnp.concatenate([y3[:, part(half, SEP)], minus], axis=1), stack_of(blk, side, 2, 2))
        two = dot(jnp.concatenate([y2[:, part(half, SEP)], minus], axis=1), stack_of(blk, side, 0, 2))
        third = one if third is None else third + one
        second = two if second is None else second + two
    total[...] = third
    hand_out(total, 1, chip, outs)
    wait(copies[14:])
    total[...] = second - dot(third.astype(BF), whole3[...])
    hand_out(total, 0, chip, outs)


def low_kernel(pos, own, oth, *refs):
    around, (u0, u1, u2, u3, y0, y1, same, other), outs, refs = refs[:8], refs[8:16], refs[16:20], refs[20:]
    solb, total, vals, blk, whole, sems = refs
    pairs = runs_of(own, oth, [(0, 1), (2, 7)], blk) + whole_of(2, own, oth, around, pos, whole)
    copies = start(pairs, sems)
    chip, core, quart = pos[0], pos[1], pos[3]
    for m, piece in enumerate((u0, u1, u2, u3)):
        for k in range(3):
            solb[k, part(quart ^ m, QUART), :] = piece[k]
    same[...] = solb[:, :, part(core, SEP)]
    other[...] = solb[:, :, part(1 - core, SEP)]
    wait(copies[:4])
    first = zeroth = None
    for side, half in enumerate((core, 1 - core)):
        vals[:, 0:SEP] = y1[:, part(half, SEP)]
        for k in range(3):
            vals[:, SEP * (k + 1) : SEP * (k + 2)] = -solb[k, :, part(half, SEP)]
        one = dot(vals[...], stack_of(blk, side, 4, 4))
        both = jnp.concatenate([y0[:, part(half, SEP)], vals[:, SEP:]], axis=1)
        two = dot(both, stack_of(blk, side, 0, 4))
        first = one if first is None else first + one
        zeroth = two if zeroth is None else zeroth + two
    total[...] = first
    hand_out(total, 1, chip, outs)
    wait(copies[4:])
    total[...] = zeroth - dot(first.astype(BF), whole[...])
    hand_out(total, 0, chip, outs)


def spread(x_anc, t, group, first, others):
    x_anc[t, :, part(group, COLS)] = first.T
    for m in range(1, 4):
        x_anc[t, :, part(group ^ m, COLS)] = others[m - 1].astype(F32).T


def rest_kernel(pos, pattern, rhs, inv, coup, upper, up1, up2, up3, rest, x_anc, solved, cm):
    for k in range(SUPERS):
        rows = pl.ds(k * SEP, SEP)
        rest[rows, :] = dot(inv[k], rhs[rows, :])
    for t in range(3):
        spread(x_anc, t, pos[2], upper[t].astype(F32), (up1[t], up2[t], up3[t]))
        solved[...] = x_anc[t].astype(BF)
        masked_into(cm, coup, pattern, t + 2)
        rest[...] -= dot(cm[...], solved[...])


def final_kernel(pos, pattern, inv, coup, sol01, got1, got2, got3, rest, anc_up, *refs):
    leaf_out, anc_out, solved, cm, x_leaf, x_anc, sems = refs
    copies = []

    def put(source, target):
        one = pltpu.make_async_copy(source, target, sems.at[len(copies)])
        one.start()
        copies.append(one)

    put(anc_up, anc_out.at[pl.ds(2, 3)])
    for t in range(2):
        first = sol01[t, :, part(pos[1], SEP)]
        spread(x_anc, t, pos[2], first, (got1[t], got2[t], got3[t]))
        put(x_anc.at[t], anc_out.at[t])
        solved[t * SEP : (t + 1) * SEP, :] = x_anc[t].astype(BF)
    for t in range(2):
        masked_into(cm.at[:, pl.ds(t * SEP, SEP)], coup, pattern, t)
    for k in range(SUPERS):
        rows = pl.ds(k * SEP, SEP)
        leaf_vb = (rest[rows, :] - dot(cm[rows, :], solved[...])).astype(BF)
        x_leaf[rows, :] = dot_tn(inv[k], leaf_vb)
        put(x_leaf.at[rows], leaf_out.at[rows])
    wait(copies)


def call(kernel, name, places, outs, scratch, sems, *args, mib=MIB, cost=None):
    shapes = [jax.ShapeDtypeStruct(dims, dtype) for dims, dtype in outs]
    scratch = [pltpu.VMEM(dims, dtype) for dims, dtype in scratch]
    if sems:
        scratch.append(pltpu.SemaphoreType.DMA((sems,)))
    here, there = places.split(":")
    return pl.pallas_call(
        kernel,
        out_shape=shapes,
        in_specs=[PLACES[p] for p in here],
        out_specs=[PLACES[there]] * len(outs),
        scratch_shapes=scratch,
        compiler_params=pltpu.CompilerParams(vmem_limit_bytes=mib * 1024 * 1024),
        cost_estimate=cost,
        name=name,
    )(*args)


def add(*values):
    return functools.reduce(jnp.add, [v.astype(F32) for v in values])


def body(leaf_rhs, leaf_inv, coupling, pattern, anc_rhs, anc_blocks):
    layer, row = lax.axis_index("layer"), lax.axis_index("row")
    chip, core = row // 2, row % 2
    flip = core == 1
    pos = jnp.stack([chip, core, (layer % 2) * 2 + core, layer // 2 % 4]).astype(jnp.int32)
    coup = coupling.transpose(1, 0, 2)
    own = anc_blocks[0]

    chosen = jnp.stack([own[k] for k in WHOLE])
    pos, chosen = lax.optimization_barrier((pos, chosen))
    oth = send_xor(own, 1)
    right, left = send_ring(chosen, 1), send_ring(chosen, 3)

    keep0, send0, yb = call(
        leaf_kernel,
        "leaf_forward",
        "ssaaaa:v",
        [((2, SEP, COLS), F32), ((2, SEP, COLS), BF), ((1024, 512), BF)],
        [((SEP, 512), F32), ((1024, SEP), BF), ((1024, 512), BF), ((SUPERS, SEP, SEP), BF)]
        + [((1, 1024, SEP), BF), ((SEP, 512), F32)],
        4,
        *(pos, pattern, leaf_rhs, leaf_inv, coup, anc_rhs[0]),
        mib=LEAF_MIB,
    )
    got0 = send_xor(send0, 8)
    keep, send = call(
        upper_kernel,
        "leaf_upper",
        "ssaav:v",
        [((4, 2, SEP, COLS), F32), ((4, 2, SEP, COLS), BF)],
        [((SEP, 512), F32), ((1024, SEP), BF), ((LEVELS, 1024, SEP), BF), ((LEVELS, SEP, 512), F32)],
        8,
        *(pos, pattern, coup, anc_rhs[0], yb),
        mib=UPPER_MIB,
    )
    near = add(keep0[0], got0[0])
    far = send_xor(add(keep0[1], got0[1]).astype(BF), 1).astype(F32)
    got_layer = send_xor(send, 8)
    got_core = send_xor(add(keep[:, 1], got_layer[:, 1]).astype(BF), 1)
    v = jnp.concatenate([jnp.where(flip, far, near), jnp.where(flip, near, far)]).astype(BF)
    v, oth, right, left = lax.optimization_barrier((v, oth, right, left))

    long = ((ANC, COLS), BF)
    y0, pend, v = call(
        zeroth_kernel,
        "forward_level0",
        "saavvvvvvv:v",
        [((COLS, ROWS), BF), ((4, ROWS, COLS), F32), ((ROWS, COLS), BF)],
        [long, ((2, 5, SEP, ANC), BF)],
        2,
        *(pos, own, oth, *ring(v), keep, got_layer, got_core),
    )
    v, right, left = lax.optimization_barrier((v, right, left))
    swapped = [send_xor(right, 1), send_xor(left, 1)]
    y1, mine, *pieces = call(
        first_kernel,
        "forward_level1",
        "saavvvvv:v",
        [((COLS, ROWS), BF), ((3, QUART, ROWS), F32)] + [((3, QUART, ROWS), BF)] * 3,
        [long, ((3, COLS, ROWS), F32), ((2, 4, SEP, ANC), BF)],
        2,
        *(pos, own, oth, *ring(v), pend),
    )
    middle = SEP // 2
    pieces, low, high, right, left, swapped = lax.optimization_barrier(
        (pieces, right[:, :middle], left[:, middle:], right, left, swapped)
    )
    low, high = send_ring(low, 1), send_ring(high, 3)
    got = [send_xor(pieces[m - 1], 16 * m) for m in (2, 3, 1)]
    pend = add(mine, *got)
    v = pend[:2].astype(BF)
    v, y1, low, high = lax.optimization_barrier((v, y1, low, high))
    around = [right, left, low, high] + swapped + [send_xor(low, 1), send_xor(high, 1)]
    thin, wide = ((QUART, ANC), BF), ((ANC, ANC), BF)
    y2, vy, v4 = call(
        middle_kernel,
        "forward_levels23",
        "s" + "a" * 10 + "v" * 5 + ":v",
        [((QUART, ROWS), BF), ((2, QUART, ROWS), BF), ((QUART, ROWS), BF)],
        [thin, thin, ((2, 4, SEP, ANC), BF), wide],
        14,
        *(pos, own, oth, *around, *ring(v), pend[2]),
    )
    got = send_xor(vy, 64)
    z4 = add(v4, got[0], send_xor(v4, 128), send_xor(v4, 192)).astype(BF)
    y3 = add(vy[1], got[1]).astype(BF)
    sol4, *outs = call(
        top_kernel,
        "top_levels",
        "s" + "a" * 10 + "v" * 6 + ":v",
        [((QUART, ROWS), BF), ((2, QUART, ROWS), F32)] + [((2, QUART, ROWS), BF)] * 3,
        [thin, ((QUART, ANC), F32), ((2, 4, SEP, ANC), BF), wide, wide],
        24,
        *(pos, own, oth, *around, *ring(z4), y2, y3),
    )
    sol23 = add(outs[0], *[send_ring(outs[d], d) for d in (2, 1, 3)])
    upper = jnp.concatenate([sol23.astype(BF), sol4[None]])
    y1 = add(y1, send_xor(y1, 16)).astype(BF)
    across = {m: send_xor(upper, 16 * m) for m in (1, 3, 2)}
    same, other, *outs = call(
        low_kernel,
        "low_levels",
        "s" + "a" * 10 + "v" * 6 + ":v",
        [((3, COLS, SEP), BF)] * 2 + [((2, COLS, ROWS), F32)] + [((2, COLS, ROWS), BF)] * 3,
        [((3, COLS, ROWS), BF), ((COLS, ANC), F32), ((COLS, 4 * SEP), BF), ((2, 8, SEP, ANC), BF), wide],
        14,
        *(pos, own, oth, *around, upper, *[across[m] for m in (1, 2, 3)], y0, y1),
    )
    sol01 = add(outs[0], *[send_ring(outs[d], d) for d in (2, 1, 3)])
    ups = [send_xor(other, 1), send_xor(same, 8), send_xor(other, 9)]
    sol01, *ups = lax.optimization_barrier((sol01, *ups))
    lower, higher = sol01[..., :SEP].astype(BF), sol01[..., SEP:].astype(BF)
    home, away = jnp.where(flip, higher, lower), jnp.where(flip, lower, higher)
    got = [send_xor(away, 1), send_xor(home, 8), send_xor(away, 9)]
    rest, anc_up = call(
        rest_kernel,
        "leaf_rest",
        "ssvvvvvvv:v",
        [((1024, 512), F32), ((3, SEP, 512), F32)],
        [((SEP, 512), BF), ((1024, SEP), BF)],
        0,
        *(pos, pattern, leaf_rhs, leaf_inv, coup, same, *ups),
    )
    x_leaf, x_anc = call(
        final_kernel,
        "leaf_backward",
        "ssvvvvvvvv:a",
        [((1024, 512), F32), ((LEVELS, SEP, 512), F32)],
        [((2 * SEP, 512), BF), ((1024, 2 * SEP), BF), ((1024, 512), F32), ((2, SEP, 512), F32)],
        11,
        *(pos, pattern, leaf_inv, coup, sol01, *got, rest, anc_up),
    )
    return x_leaf, x_anc[None]


def solution(mesh):
    placed = (
        P(("layer", "row"), None),
        P(("layer", "row"), None, None),
        P(("layer", "row"), None, None),
        P(("layer", "row"), None),
        P("layer", None, "row", None),
        P("layer", None, "row", None),
    )
    return jax.shard_map(
        body,
        mesh=mesh,
        in_specs=placed,
        out_specs=(P(("layer", "row"), None), P("layer", None, "row", None)),
        check_vma=False,
    )
```

```python
import functools

import jax
import jax.numpy as jnp
from jax import lax
from jax.experimental import pallas as pl
from jax.experimental.pallas import tpu as pltpu
from jax.sharding import PartitionSpec as P

BF = jnp.bfloat16
F32 = jnp.float32
LEVELS = 5
SUPERS = 8
SEP = 128
ROWS = 256
ANC = 1024
COLS = 128
QUART = 32
MIB = 52
UPPER_MIB = 58
LEAF_MIB = 58
CHIPS = 4
AXES = ("layer", "row")
PLACES = {
    "s": pl.BlockSpec(memory_space=pltpu.SMEM),
    "v": pl.BlockSpec(memory_space=pltpu.VMEM),
    "a": pl.BlockSpec(memory_space=pl.ANY),
}
WHOLE = (10, 14, 1)


def block_start(level):
    return level * LEVELS - level * (level - 1) // 2


def devices():
    return lax.axis_size("layer") * lax.axis_size("row")


def send_xor(value, mask):
    return lax.ppermute(value, AXES, [(i, i ^ mask) for i in range(devices())])


def send_ring(value, step):
    pairs = [(i, (i & ~6) | ((((i >> 1 & 3) + step) % CHIPS) << 1)) for i in range(devices())]
    return lax.ppermute(value, AXES, pairs)


def ring(value):
    got = {d: send_ring(value, d) for d in (1, 3, 2)}
    return [value] + [got[d] for d in (1, 2, 3)]


def part(start, size):
    return pl.ds(pl.multiple_of(start * size, size), size)


def dot(a, b):
    return jnp.dot(a, b, preferred_element_type=F32)


def dot_nt(a, b):
    return lax.dot_general(a, b, (((1,), (1,)), ((), ())), preferred_element_type=F32)


def dot_tn(a, b):
    return lax.dot_general(a, b, (((0,), (0,)), ((), ())), preferred_element_type=F32)


def start(pairs, sems):
    copies = [pltpu.make_async_copy(a, b, sems.at[i]) for i, (a, b) in enumerate(pairs)]
    for one in copies:
        one.start()
    return copies


def wait(copies):
    for one in copies:
        one.wait()


def runs_of(own, oth, runs, blk):
    pairs, at = [], 0
    for first, count in runs:
        for side, blocks in enumerate((own, oth)):
            pairs.append((blocks.at[pl.ds(first, count)], blk.at[side, pl.ds(at, count)]))
        at += count
    return pairs


def whole_of(index, own, oth, around, pos, target):
    chip, core = pos[0], pos[1]
    pairs = []
    for side, c in enumerate((core, 1 - core)):
        right, left, low, high = around[4 * side : 4 * side + 4]
        near = (own, oth)[side].at[WHOLE[index]]
        for source, d in ((near, 0), (right.at[index], 1), (left.at[index], 3)):
            row = 2 * ((chip + CHIPS - d) % CHIPS) + c
            pairs.append((source, target.at[part(row, SEP)]))
        row = 2 * (2 * ((chip + 2) % CHIPS) + c)
        pairs.append((low.at[index], target.at[part(row, SEP // 2)]))
        pairs.append((high.at[index], target.at[part(row + 1, SEP // 2)]))
    return pairs


def stack_of(blk, side, first, count):
    return blk[side, first : first + count].reshape(count * SEP, ANC)


def masked_into(cm, coup, pattern, t):
    for k in range(SUPERS):
        rows = pl.ds(k * SEP, SEP)
        keep = pattern[k, t].astype(F32)
        cm[rows, :] = (coup[t, rows, :].astype(F32) * keep).astype(BF)


def split_share(share, group, keep, send):
    for m in range(2):
        keep[m] = share[:, part(group ^ m, COLS)]
        send[m] = share[:, part(group ^ (2 + m), COLS)].astype(BF)


def leaf_kernel(pos, pattern, rhs_in, inv_in, coup_in, anc_in, keep, send, yb, share, cm, rhs, inv, coup, anc, sems):
    pairs = [(inv_in, inv), (rhs_in, rhs), (coup_in.at[pl.ds(0, 1)], coup), (anc_in.at[0], anc)]
    copies = start(pairs, sems)
    wait(copies[:2])
    for k in range(SUPERS):
        rows = pl.ds(k * SEP, SEP)
        yb[rows, :] = dot(inv[k], rhs[rows, :]).astype(BF)
    wait(copies[2:])
    masked_into(cm, coup, pattern, 0)
    share[...] = anc[...] - dot_tn(cm[...], yb[...])
    split_share(share, pos[2], keep, send)


def upper_kernel(pos, pattern, coup_in, anc_in, yb, keep, send, share, cm, coup, anc, sems):
    pairs = []
    for t in range(1, LEVELS):
        pairs += [(coup_in.at[t], coup.at[t]), (anc_in.at[t], anc.at[t])]
    copies = start(pairs, sems)
    for t in range(1, LEVELS):
        wait(copies[2 * t - 2 : 2 * t])
        masked_into(cm, coup, pattern, t)
        share[...] = anc[t] - dot_tn(cm[...], yb[...])
        split_share(share, pos[2], keep.at[t - 1], send.at[t - 1])


def zeroth_kernel(pos, own, oth, z0, z1, z2, z3, keep, got_layer, got_core, y_out, pend, v_out, zabs, blk, sems):
    copies = start(runs_of(own, oth, [(0, 5)], blk), sems)
    chip, core = pos[0], pos[1]
    for d, z in enumerate((z0, z1, z2, z3)):
        zabs[part((chip + CHIPS - d) % CHIPS, ROWS), :] = z[...]
    for side, half in enumerate((core, 1 - core)):
        copies[side].wait()
        product = dot(stack_of(blk, side, 0, 5), zabs[...])
        y_out[:, part(half, SEP)] = product[:SEP].T.astype(BF)
        for k in range(4):
            if side == 0:
                base = keep[k, 0] + got_layer[k, 0].astype(F32)
            else:
                base = got_core[k].astype(F32)
            after = base - product[(k + 1) * SEP : (k + 2) * SEP]
            pend[k, part(half, SEP), :] = after
            if k == 0:
                v_out[part(half, SEP), :] = after.astype(BF)


def first_kernel(pos, own, oth, z0, z1, z2, z3, pend, y_out, mine, s1, s2, s3, zabs, turned, blk, sems):
    copies = start(runs_of(own, oth, [(5, 4)], blk), sems)
    chip, core, quart = pos[0], pos[1], pos[3]
    for d, z in enumerate((z0, z1, z2, z3)):
        zabs[part((chip + CHIPS - d) % CHIPS, ROWS), :] = z[...]
    for side, half in enumerate((core, 1 - core)):
        copies[side].wait()
        product = dot(stack_of(blk, side, 0, 4), zabs[...])
        y_out[:, part(half, SEP)] = product[:SEP].T.astype(BF)
        for k in range(3):
            after = pend[k + 1, part(half, SEP), :] - product[(k + 1) * SEP : (k + 2) * SEP]
            turned[k, :, part(half, SEP)] = after.T
    for m, out in enumerate((mine, s1, s2, s3)):
        for k in range(3):
            out[k] = turned[k, part(quart ^ m, QUART), :].astype(out.dtype)


def middle_kernel(pos, own, oth, *refs):
    around, (z0, z1, z2, z3, pend, y2, vy, v4), refs = refs[:8], refs[8:16], refs[16:]
    za, zb, blk, whole, sems = refs
    pairs = whole_of(0, own, oth, around, pos, whole) + runs_of(own, oth, [(9, 1), (11, 3)], blk)
    copies = start(pairs, sems)
    chip, core = pos[0], pos[1]
    for d, z in enumerate((z0, z1, z2, z3)):
        place = part((chip + CHIPS - d) % CHIPS, ROWS)
        za[:, place] = z[0]
        zb[:, place] = z[1]
    wait(copies[:10])
    zb[...] = (zb[...].astype(F32) - dot_nt(za[...], whole[...])).astype(BF)
    wait(copies[10:])
    for side, half in enumerate((core, 1 - core)):
        two = dot_nt(za[...], stack_of(blk, side, 0, 2))
        three = dot_nt(zb[...], stack_of(blk, side, 2, 2))
        y2[:, part(half, SEP)] = two[:, :SEP].astype(BF)
        vy[1, :, part(half, SEP)] = three[:, :SEP].astype(BF)
        after = (pend[:, part(half, SEP)] - two[:, SEP:] - three[:, SEP:]).astype(BF)
        vy[0, :, part(half, SEP)] = after
        v4[:, part(half, SEP)] = after


def hand_out(total, level_at, chip, outs):
    for d, out in enumerate(outs):
        out[level_at] = total[:, part((chip + d) % CHIPS, ROWS)].astype(out.dtype)


def top_kernel(pos, own, oth, *refs):
    around, (z0, z1, z2, z3, y2, y3, solb), outs, refs = refs[:8], refs[8:15], refs[15:19], refs[19:]
    za, total, blk, whole4, whole3, sems = refs
    pairs = whole_of(1, own, oth, around, pos, whole4) + runs_of(own, oth, [(9, 1), (11, 3)], blk)
    pairs += whole_of(0, own, oth, around, pos, whole3)
    copies = start(pairs, sems)
    chip, core = pos[0], pos[1]
    for d, z in enumerate((z0, z1, z2, z3)):
        za[:, part((chip + CHIPS - d) % CHIPS, ROWS)] = z[...]
    wait(copies[:10])
    y4 = dot_nt(za[...], whole4[...]).astype(BF)
    solb[...] = dot(y4, whole4[:, part(chip, ROWS)]).astype(BF)
    wait(copies[10:14])
    third = second = None
    for side, half in enumerate((core, 1 - core)):
        minus = -solb[:, part(half, SEP)]
        one = dot(jnp.concatenate([y3[:, part(half, SEP)], minus], axis=1), stack_of(blk, side, 2, 2))
        two = dot(jnp.concatenate([y2[:, part(half, SEP)], minus], axis=1), stack_of(blk, side, 0, 2))
        third = one if third is None else third + one
        second = two if second is None else second + two
    total[...] = third
    hand_out(total, 1, chip, outs)
    wait(copies[14:])
    total[...] = second - dot(third.astype(BF), whole3[...])
    hand_out(total, 0, chip, outs)


def low_kernel(pos, own, oth, *refs):
    around, (u0, u1, u2, u3, y0, y1, same, other), outs, refs = refs[:8], refs[8:16], refs[16:20], refs[20:]
    solb, total, vals, blk, whole, sems = refs
    pairs = runs_of(own, oth, [(0, 1), (2, 7)], blk) + whole_of(2, own, oth, around, pos, whole)
    copies = start(pairs, sems)
    chip, core, quart = pos[0], pos[1], pos[3]
    for m, piece in enumerate((u0, u1, u2, u3)):
        for k in range(3):
            solb[k, part(quart ^ m, QUART), :] = piece[k]
    same[...] = solb[:, :, part(core, SEP)]
    other[...] = solb[:, :, part(1 - core, SEP)]
    wait(copies[:4])
    first = zeroth = None
    for side, half in enumerate((core, 1 - core)):
        vals[:, 0:SEP] = y1[:, part(half, SEP)]
        for k in range(3):
            vals[:, SEP * (k + 1) : SEP * (k + 2)] = -solb[k, :, part(half, SEP)]
        one = dot(vals[...], stack_of(blk, side, 4, 4))
        both = jnp.concatenate([y0[:, part(half, SEP)], vals[:, SEP:]], axis=1)
        two = dot(both, stack_of(blk, side, 0, 4))
        first = one if first is None else first + one
        zeroth = two if zeroth is None else zeroth + two
    total[...] = first
    hand_out(total, 1, chip, outs)
    wait(copies[4:])
    total[...] = zeroth - dot(first.astype(BF), whole[...])
    hand_out(total, 0, chip, outs)


def spread(x_anc, t, group, first, others):
    x_anc[t, :, part(group, COLS)] = first.T
    for m in range(1, 4):
        x_anc[t, :, part(group ^ m, COLS)] = others[m - 1].astype(F32).T


def rest_kernel(pos, pattern, rhs, inv, coup, upper, up1, up2, up3, rest, x_anc, solved, cm):
    for t in range(3):
        spread(x_anc, t, pos[2], upper[t].astype(F32), (up1[t], up2[t], up3[t]))
        solved[t * SEP : (t + 1) * SEP, :] = x_anc[t].astype(BF)
        masked_into(cm.at[:, pl.ds(t * SEP, SEP)], coup, pattern, t + 2)
    for k in range(SUPERS):
        rows = pl.ds(k * SEP, SEP)
        rest[rows, :] = dot(inv[k], rhs[rows, :]) - dot(cm[rows, :], solved[...])


def final_kernel(pos, pattern, inv, coup, sol01, got1, got2, got3, rest, anc_up, *refs):
    leaf_out, anc_out, solved, cm, x_leaf, x_anc, sems = refs
    copies = []

    def put(source, target):
        one = pltpu.make_async_copy(source, target, sems.at[len(copies)])
        one.start()
        copies.append(one)

    put(anc_up, anc_out.at[pl.ds(2, 3)])
    for t in range(2):
        first = sol01[t, :, part(pos[1], SEP)]
        spread(x_anc, t, pos[2], first, (got1[t], got2[t], got3[t]))
        put(x_anc.at[t], anc_out.at[t])
        solved[t * SEP : (t + 1) * SEP, :] = x_anc[t].astype(BF)
    for t in range(2):
        masked_into(cm.at[:, pl.ds(t * SEP, SEP)], coup, pattern, t)
    for k in range(SUPERS):
        rows = pl.ds(k * SEP, SEP)
        leaf_vb = (rest[rows, :] - dot(cm[rows, :], solved[...])).astype(BF)
        x_leaf[rows, :] = dot_tn(inv[k], leaf_vb)
        put(x_leaf.at[rows], leaf_out.at[rows])
    wait(copies)


def call(kernel, name, places, outs, scratch, sems, *args, mib=MIB, cost=None):
    shapes = [jax.ShapeDtypeStruct(dims, dtype) for dims, dtype in outs]
    scratch = [pltpu.VMEM(dims, dtype) for dims, dtype in scratch]
    if sems:
        scratch.append(pltpu.SemaphoreType.DMA((sems,)))
    here, there = places.split(":")
    return pl.pallas_call(
        kernel,
        out_shape=shapes,
        in_specs=[PLACES[p] for p in here],
        out_specs=[PLACES[there]] * len(outs),
        scratch_shapes=scratch,
        compiler_params=pltpu.CompilerParams(vmem_limit_bytes=mib * 1024 * 1024),
        cost_estimate=cost,
        name=name,
    )(*args)


def add(*values):
    return functools.reduce(jnp.add, [v.astype(F32) for v in values])


def body(leaf_rhs, leaf_inv, coupling, pattern, anc_rhs, anc_blocks):
    layer, row = lax.axis_index("layer"), lax.axis_index("row")
    chip, core = row // 2, row % 2
    flip = core == 1
    pos = jnp.stack([chip, core, (layer % 2) * 2 + core, layer // 2 % 4]).astype(jnp.int32)
    coup = coupling.transpose(1, 0, 2)
    own = anc_blocks[0]

    chosen = jnp.stack([own[k] for k in WHOLE])
    pos, chosen = lax.optimization_barrier((pos, chosen))
    oth = send_xor(own, 1)
    right, left = send_ring(chosen, 1), send_ring(chosen, 3)

    keep0, send0, yb = call(
        leaf_kernel,
        "leaf_forward",
        "ssaaaa:v",
        [((2, SEP, COLS), F32), ((2, SEP, COLS), BF), ((1024, 512), BF)],
        [((SEP, 512), F32), ((1024, SEP), BF), ((1024, 512), BF), ((SUPERS, SEP, SEP), BF)]
        + [((1, 1024, SEP), BF), ((SEP, 512), F32)],
        4,
        *(pos, pattern, leaf_rhs, leaf_inv, coup, anc_rhs[0]),
        mib=LEAF_MIB,
    )
    got0 = send_xor(send0, 8)
    keep, send = call(
        upper_kernel,
        "leaf_upper",
        "ssaav:v",
        [((4, 2, SEP, COLS), F32), ((4, 2, SEP, COLS), BF)],
        [((SEP, 512), F32), ((1024, SEP), BF), ((LEVELS, 1024, SEP), BF), ((LEVELS, SEP, 512), F32)],
        8,
        *(pos, pattern, coup, anc_rhs[0], yb),
        mib=UPPER_MIB,
    )
    near = add(keep0[0], got0[0])
    far = send_xor(add(keep0[1], got0[1]).astype(BF), 1).astype(F32)
    far, oth, right, left = lax.optimization_barrier((far, oth, right, left))
    got_layer = send_xor(send, 8)
    got_core = send_xor(add(keep[:, 1], got_layer[:, 1]).astype(BF), 1)
    v = jnp.concatenate([jnp.where(flip, far, near), jnp.where(flip, near, far)]).astype(BF)

    long = ((ANC, COLS), BF)
    y0, pend, v = call(
        zeroth_kernel,
        "forward_level0",
        "saavvvvvvv:v",
        [((COLS, ROWS), BF), ((4, ROWS, COLS), F32), ((ROWS, COLS), BF)],
        [long, ((2, 5, SEP, ANC), BF)],
        2,
        *(pos, own, oth, *ring(v), keep, got_layer, got_core),
    )
    v, right, left = lax.optimization_barrier((v, right, left))
    swapped = [send_xor(right, 1), send_xor(left, 1)]
    y1, mine, *pieces = call(
        first_kernel,
        "forward_level1",
        "saavvvvv:v",
        [((COLS, ROWS), BF), ((3, QUART, ROWS), F32)] + [((3, QUART, ROWS), BF)] * 3,
        [long, ((3, COLS, ROWS), F32), ((2, 4, SEP, ANC), BF)],
        2,
        *(pos, own, oth, *ring(v), pend),
    )
    middle = SEP // 2
    pieces, low, high, right, left, swapped = lax.optimization_barrier(
        (pieces, right[:, :middle], left[:, middle:], right, left, swapped)
    )
    low, high = send_ring(low, 1), send_ring(high, 3)
    got = [send_xor(pieces[m - 1], 16 * m) for m in (2, 3, 1)]
    pend = add(mine, *got)
    v = pend[:2].astype(BF)
    v, y1, low, high = lax.optimization_barrier((v, y1, low, high))
    around = [right, left, low, high] + swapped + [send_xor(low, 1), send_xor(high, 1)]
    thin, wide = ((QUART, ANC), BF), ((ANC, ANC), BF)
    y2, vy, v4 = call(
        middle_kernel,
        "forward_levels23",
        "s" + "a" * 10 + "v" * 5 + ":v",
        [((QUART, ROWS), BF), ((2, QUART, ROWS), BF), ((QUART, ROWS), BF)],
        [thin, thin, ((2, 4, SEP, ANC), BF), wide],
        14,
        *(pos, own, oth, *around, *ring(v), pend[2]),
    )
    got = send_xor(vy, 64)
    z4 = add(v4, got[0], send_xor(v4, 128), send_xor(v4, 192)).astype(BF)
    y3 = add(vy[1], got[1]).astype(BF)
    sol4, *outs = call(
        top_kernel,
        "top_levels",
        "s" + "a" * 10 + "v" * 6 + ":v",
        [((QUART, ROWS), BF), ((2, QUART, ROWS), F32)] + [((2, QUART, ROWS), BF)] * 3,
        [thin, ((QUART, ANC), F32), ((2, 4, SEP, ANC), BF), wide, wide],
        24,
        *(pos, own, oth, *around, *ring(z4), y2, y3),
    )
    sol23 = add(outs[0], *[send_ring(outs[d], d) for d in (2, 1, 3)])
    upper = jnp.concatenate([sol23.astype(BF), sol4[None]])
    y1 = add(y1, send_xor(y1, 16)).astype(BF)
    across = {m: send_xor(upper, 16 * m) for m in (1, 3, 2)}
    same, other, *outs = call(
        low_kernel,
        "low_levels",
        "s" + "a" * 10 + "v" * 6 + ":v",
        [((3, COLS, SEP), BF)] * 2 + [((2, COLS, ROWS), F32)] + [((2, COLS, ROWS), BF)] * 3,
        [((3, COLS, ROWS), BF), ((COLS, ANC), F32), ((COLS, 4 * SEP), BF), ((2, 8, SEP, ANC), BF), wide],
        14,
        *(pos, own, oth, *around, upper, *[across[m] for m in (1, 2, 3)], y0, y1),
    )
    sol01 = add(outs[0], *[send_ring(outs[d], d) for d in (2, 1, 3)])
    ups = [send_xor(other, 1), send_xor(same, 8), send_xor(other, 9)]
    lower, higher = sol01[..., :SEP].astype(BF), sol01[..., SEP:].astype(BF)
    home, away = jnp.where(flip, higher, lower), jnp.where(flip, lower, higher)
    got = [send_xor(away, 1), send_xor(home, 8), send_xor(away, 9)]
    rest, anc_up = call(
        rest_kernel,
        "leaf_rest",
        "ssvvvvvvv:v",
        [((1024, 512), F32), ((3, SEP, 512), F32)],
        [((3 * SEP, 512), BF), ((1024, 3 * SEP), BF)],
        0,
        *(pos, pattern, leaf_rhs, leaf_inv, coup, same, *ups),
    )
    x_leaf, x_anc = call(
        final_kernel,
        "leaf_backward",
        "ssvvvvvvvv:a",
        [((1024, 512), F32), ((LEVELS, SEP, 512), F32)],
        [((2 * SEP, 512), BF), ((1024, 2 * SEP), BF), ((1024, 512), F32), ((2, SEP, 512), F32)],
        11,
        *(pos, pattern, leaf_inv, coup, sol01, *got, rest, anc_up),
    )
    return x_leaf, x_anc[None]


def solution(mesh):
    placed = (
        P(("layer", "row"), None),
        P(("layer", "row"), None, None),
        P(("layer", "row"), None, None),
        P(("layer", "row"), None),
        P("layer", None, "row", None),
        P("layer", None, "row", None),
    )
    return jax.shard_map(
        body,
        mesh=mesh,
        in_specs=placed,
        out_specs=(P(("layer", "row"), None), P("layer", None, "row", None)),
        check_vma=False,
    )
```

```python
import functools

import jax
import jax.numpy as jnp
from jax import lax
from jax.experimental import pallas as pl
from jax.experimental.pallas import tpu as pltpu
from jax.sharding import PartitionSpec as P

BF = jnp.bfloat16
F32 = jnp.float32
LEVELS = 5
SUPERS = 8
SEP = 128
ROWS = 256
ANC = 1024
COLS = 128
QUART = 32
MIB = 52
UPPER_MIB = 58
LEAF_MIB = 58
CHIPS = 4
AXES = ("layer", "row")
PLACES = {
    "s": pl.BlockSpec(memory_space=pltpu.SMEM),
    "v": pl.BlockSpec(memory_space=pltpu.VMEM),
    "a": pl.BlockSpec(memory_space=pl.ANY),
}
WHOLE = (10, 14, 1)


def block_start(level):
    return level * LEVELS - level * (level - 1) // 2


def devices():
    return lax.axis_size("layer") * lax.axis_size("row")


def send_xor(value, mask):
    return lax.ppermute(value, AXES, [(i, i ^ mask) for i in range(devices())])


def send_ring(value, step):
    pairs = [(i, (i & ~6) | ((((i >> 1 & 3) + step) % CHIPS) << 1)) for i in range(devices())]
    return lax.ppermute(value, AXES, pairs)


def ring(value):
    got = {d: send_ring(value, d) for d in (1, 3, 2)}
    return [value] + [got[d] for d in (1, 2, 3)]


def part(start, size):
    return pl.ds(pl.multiple_of(start * size, size), size)


def dot(a, b):
    return jnp.dot(a, b, preferred_element_type=F32)


def dot_nt(a, b):
    return lax.dot_general(a, b, (((1,), (1,)), ((), ())), preferred_element_type=F32)


def dot_tn(a, b):
    return lax.dot_general(a, b, (((0,), (0,)), ((), ())), preferred_element_type=F32)


def start(pairs, sems):
    copies = [pltpu.make_async_copy(a, b, sems.at[i]) for i, (a, b) in enumerate(pairs)]
    for one in copies:
        one.start()
    return copies


def wait(copies):
    for one in copies:
        one.wait()


def runs_of(own, oth, runs, blk):
    pairs, at = [], 0
    for first, count in runs:
        for side, blocks in enumerate((own, oth)):
            pairs.append((blocks.at[pl.ds(first, count)], blk.at[side, pl.ds(at, count)]))
        at += count
    return pairs


def whole_of(index, own, oth, around, pos, target):
    chip, core = pos[0], pos[1]
    pairs = []
    for side, c in enumerate((core, 1 - core)):
        right, left, low, high = around[4 * side : 4 * side + 4]
        near = (own, oth)[side].at[WHOLE[index]]
        for source, d in ((near, 0), (right.at[index], 1), (left.at[index], 3)):
            row = 2 * ((chip + CHIPS - d) % CHIPS) + c
            pairs.append((source, target.at[part(row, SEP)]))
        row = 2 * (2 * ((chip + 2) % CHIPS) + c)
        pairs.append((low.at[index], target.at[part(row, SEP // 2)]))
        pairs.append((high.at[index], target.at[part(row + 1, SEP // 2)]))
    return pairs


def stack_of(blk, side, first, count):
    return blk[side, first : first + count].reshape(count * SEP, ANC)


def runs_kernel(runs, pos, own, oth, blk, sems):
    wait(start(runs_of(own, oth, runs, blk), sems))


def whole_kernel(index, pos, own, oth, *refs):
    around, whole, sems = refs[:8], refs[8], refs[9]
    wait(start(whole_of(index, own, oth, around, pos, whole), sems))


def masked_into(cm, coup, pattern, t):
    for k in range(SUPERS):
        rows = pl.ds(k * SEP, SEP)
        keep = pattern[k, t].astype(F32)
        cm[rows, :] = (coup[t, rows, :].astype(F32) * keep).astype(BF)


def split_share(share, group, keep, send):
    for m in range(2):
        keep[m] = share[:, part(group ^ m, COLS)]
        send[m] = share[:, part(group ^ (2 + m), COLS)].astype(BF)


def leaf_kernel(pos, pattern, rhs_in, inv_in, coup_in, anc_in, keep, send, yb, share, cm, rhs, inv, coup, anc, sems):
    pairs = [(inv_in, inv), (rhs_in, rhs), (coup_in.at[pl.ds(0, 1)], coup), (anc_in.at[0], anc)]
    copies = start(pairs, sems)
    wait(copies[:2])
    for k in range(SUPERS):
        rows = pl.ds(k * SEP, SEP)
        yb[rows, :] = dot(inv[k], rhs[rows, :]).astype(BF)
    wait(copies[2:])
    masked_into(cm, coup, pattern, 0)
    share[...] = anc[...] - dot_tn(cm[...], yb[...])
    split_share(share, pos[2], keep, send)


def upper_kernel(pos, pattern, coup_in, anc_in, yb, keep, send, share, cm, coup, anc, sems):
    pairs = []
    for t in range(1, LEVELS):
        pairs += [(coup_in.at[t], coup.at[t]), (anc_in.at[t], anc.at[t])]
    copies = start(pairs, sems)
    for t in range(1, LEVELS):
        wait(copies[2 * t - 2 : 2 * t])
        masked_into(cm, coup, pattern, t)
        share[...] = anc[t] - dot_tn(cm[...], yb[...])
        split_share(share, pos[2], keep.at[t - 1], send.at[t - 1])


def zeroth_kernel(pos, blk, z0, z1, z2, z3, keep, got_layer, got_core, y_out, pend, v_out, zabs):
    chip, core = pos[0], pos[1]
    for d, z in enumerate((z0, z1, z2, z3)):
        zabs[part((chip + CHIPS - d) % CHIPS, ROWS), :] = z[...]
    for side, half in enumerate((core, 1 - core)):
        product = dot(stack_of(blk, side, 0, 5), zabs[...])
        y_out[:, part(half, SEP)] = product[:SEP].T.astype(BF)
        for k in range(4):
            if side == 0:
                base = keep[k, 0] + got_layer[k, 0].astype(F32)
            else:
                base = got_core[k].astype(F32)
            after = base - product[(k + 1) * SEP : (k + 2) * SEP]
            pend[k, part(half, SEP), :] = after
            if k == 0:
                v_out[part(half, SEP), :] = after.astype(BF)


def first_kernel(pos, blk, z0, z1, z2, z3, pend, y_out, mine, s1, s2, s3, zabs, turned):
    chip, core, quart = pos[0], pos[1], pos[3]
    for d, z in enumerate((z0, z1, z2, z3)):
        zabs[part((chip + CHIPS - d) % CHIPS, ROWS), :] = z[...]
    for side, half in enumerate((core, 1 - core)):
        product = dot(stack_of(blk, side, 0, 4), zabs[...])
        y_out[:, part(half, SEP)] = product[:SEP].T.astype(BF)
        for k in range(3):
            after = pend[k + 1, part(half, SEP), :] - product[(k + 1) * SEP : (k + 2) * SEP]
            turned[k, :, part(half, SEP)] = after.T
    for m, out in enumerate((mine, s1, s2, s3)):
        for k in range(3):
            out[k] = turned[k, part(quart ^ m, QUART), :].astype(out.dtype)


def middle_kernel(pos, own, oth, *refs):
    around, (blk, z0, z1, z2, z3, pend, y2, vy, v4), refs = refs[:8], refs[8:17], refs[17:]
    za, zb, whole, sems = refs
    copies = start(whole_of(0, own, oth, around, pos, whole), sems)
    chip, core = pos[0], pos[1]
    for d, z in enumerate((z0, z1, z2, z3)):
        place = part((chip + CHIPS - d) % CHIPS, ROWS)
        za[:, place] = z[0]
        zb[:, place] = z[1]
    wait(copies)
    zb[...] = (zb[...].astype(F32) - dot_nt(za[...], whole[...])).astype(BF)
    for side, half in enumerate((core, 1 - core)):
        two = dot_nt(za[...], stack_of(blk, side, 0, 2))
        three = dot_nt(zb[...], stack_of(blk, side, 2, 2))
        y2[:, part(half, SEP)] = two[:, :SEP].astype(BF)
        vy[1, :, part(half, SEP)] = three[:, :SEP].astype(BF)
        after = (pend[:, part(half, SEP)] - two[:, SEP:] - three[:, SEP:]).astype(BF)
        vy[0, :, part(half, SEP)] = after
        v4[:, part(half, SEP)] = after


def hand_out(total, level_at, chip, outs):
    for d, out in enumerate(outs):
        out[level_at] = total[:, part((chip + d) % CHIPS, ROWS)].astype(out.dtype)


def top_kernel(pos, blk, whole4, whole3, z0, z1, z2, z3, y2, y3, solb, *refs):
    outs, (za, total) = refs[:4], refs[4:]
    chip, core = pos[0], pos[1]
    for d, z in enumerate((z0, z1, z2, z3)):
        za[:, part((chip + CHIPS - d) % CHIPS, ROWS)] = z[...]
    y4 = dot_nt(za[...], whole4[...]).astype(BF)
    solb[...] = dot(y4, whole4[:, part(chip, ROWS)]).astype(BF)
    third = second = None
    for side, half in enumerate((core, 1 - core)):
        minus = -solb[:, part(half, SEP)]
        one = dot(jnp.concatenate([y3[:, part(half, SEP)], minus], axis=1), stack_of(blk, side, 2, 2))
        two = dot(jnp.concatenate([y2[:, part(half, SEP)], minus], axis=1), stack_of(blk, side, 0, 2))
        third = one if third is None else third + one
        second = two if second is None else second + two
    total[...] = third
    hand_out(total, 1, chip, outs)
    total[...] = second - dot(third.astype(BF), whole3[...])
    hand_out(total, 0, chip, outs)


def low_kernel(pos, blk0, blk1, whole, u0, u1, u2, u3, y0, y1, same, other, *refs):
    outs, (solb, total, vals) = refs[:4], refs[4:]
    chip, core, quart = pos[0], pos[1], pos[3]
    for m, piece in enumerate((u0, u1, u2, u3)):
        for k in range(3):
            solb[k, part(quart ^ m, QUART), :] = piece[k]
    same[...] = solb[:, :, part(core, SEP)]
    other[...] = solb[:, :, part(1 - core, SEP)]
    first = zeroth = None
    for side, half in enumerate((core, 1 - core)):
        vals[:, 0:SEP] = y1[:, part(half, SEP)]
        for k in range(3):
            vals[:, SEP * (k + 1) : SEP * (k + 2)] = -solb[k, :, part(half, SEP)]
        one = dot(vals[...], stack_of(blk1, side, 0, 4))
        both = jnp.concatenate([y0[:, part(half, SEP)], vals[:, SEP:]], axis=1)
        two = dot(both, stack_of(blk0, side, 0, 4))
        first = one if first is None else first + one
        zeroth = two if zeroth is None else zeroth + two
    total[...] = first
    hand_out(total, 1, chip, outs)
    total[...] = zeroth - dot(first.astype(BF), whole[...])
    hand_out(total, 0, chip, outs)


def spread(x_anc, t, group, first, others):
    x_anc[t, :, part(group, COLS)] = first.T
    for m in range(1, 4):
        x_anc[t, :, part(group ^ m, COLS)] = others[m - 1].astype(F32).T


def rest_kernel(pos, pattern, rhs, inv, coup, upper, up1, up2, up3, rest, x_anc, solved, cm):
    for t in range(3):
        spread(x_anc, t, pos[2], upper[t].astype(F32), (up1[t], up2[t], up3[t]))
        solved[t * SEP : (t + 1) * SEP, :] = x_anc[t].astype(BF)
        masked_into(cm.at[:, pl.ds(t * SEP, SEP)], coup, pattern, t + 2)
    for k in range(SUPERS):
        rows = pl.ds(k * SEP, SEP)
        rest[rows, :] = dot(inv[k], rhs[rows, :]) - dot(cm[rows, :], solved[...])


def final_kernel(pos, pattern, inv, coup, sol01, got1, got2, got3, rest, anc_up, *refs):
    leaf_out, anc_out, solved, cm, x_leaf, x_anc, sems = refs
    copies = []

    def put(source, target):
        one = pltpu.make_async_copy(source, target, sems.at[len(copies)])
        one.start()
        copies.append(one)

    put(anc_up, anc_out.at[pl.ds(2, 3)])
    for t in range(2):
        first = sol01[t, :, part(pos[1], SEP)]
        spread(x_anc, t, pos[2], first, (got1[t], got2[t], got3[t]))
        put(x_anc.at[t], anc_out.at[t])
        solved[t * SEP : (t + 1) * SEP, :] = x_anc[t].astype(BF)
    for t in range(2):
        masked_into(cm.at[:, pl.ds(t * SEP, SEP)], coup, pattern, t)
    for k in range(SUPERS):
        rows = pl.ds(k * SEP, SEP)
        leaf_vb = (rest[rows, :] - dot(cm[rows, :], solved[...])).astype(BF)
        x_leaf[rows, :] = dot_tn(inv[k], leaf_vb)
        put(x_leaf.at[rows], leaf_out.at[rows])
    wait(copies)


def call(kernel, name, places, outs, scratch, sems, *args, mib=MIB, cost=None):
    shapes = [jax.ShapeDtypeStruct(dims, dtype) for dims, dtype in outs]
    scratch = [pltpu.VMEM(dims, dtype) for dims, dtype in scratch]
    if sems:
        scratch.append(pltpu.SemaphoreType.DMA((sems,)))
    here, there = places.split(":")
    return pl.pallas_call(
        kernel,
        out_shape=shapes,
        in_specs=[PLACES[p] for p in here],
        out_specs=[PLACES[there]] * len(outs),
        scratch_shapes=scratch,
        compiler_params=pltpu.CompilerParams(vmem_limit_bytes=mib * 1024 * 1024),
        cost_estimate=cost,
        name=name,
    )(*args)


def loading(parts):
    return pl.CostEstimate(flops=1, bytes_accessed=parts * SEP * ANC * 2, transcendentals=0)


def add(*values):
    return functools.reduce(jnp.add, [v.astype(F32) for v in values])


def body(leaf_rhs, leaf_inv, coupling, pattern, anc_rhs, anc_blocks):
    layer, row = lax.axis_index("layer"), lax.axis_index("row")
    chip, core = row // 2, row % 2
    flip = core == 1
    pos = jnp.stack([chip, core, (layer % 2) * 2 + core, layer // 2 % 4]).astype(jnp.int32)
    coup = coupling.transpose(1, 0, 2)
    own = anc_blocks[0]

    chosen = jnp.stack([own[k] for k in WHOLE])
    pos, chosen = lax.optimization_barrier((pos, chosen))
    oth = send_xor(own, 1)
    right, left = send_ring(chosen, 1), send_ring(chosen, 3)

    keep0, send0, yb = call(
        leaf_kernel,
        "leaf_forward",
        "ssaaaa:v",
        [((2, SEP, COLS), F32), ((2, SEP, COLS), BF), ((1024, 512), BF)],
        [((SEP, 512), F32), ((1024, SEP), BF), ((1024, 512), BF), ((SUPERS, SEP, SEP), BF)]
        + [((1, 1024, SEP), BF), ((SEP, 512), F32)],
        4,
        *(pos, pattern, leaf_rhs, leaf_inv, coup, anc_rhs[0]),
        mib=LEAF_MIB,
    )
    got0 = send_xor(send0, 8)
    keep, send = call(
        upper_kernel,
        "leaf_upper",
        "ssaav:v",
        [((4, 2, SEP, COLS), F32), ((4, 2, SEP, COLS), BF)],
        [((SEP, 512), F32), ((1024, SEP), BF), ((LEVELS, 1024, SEP), BF), ((LEVELS, SEP, 512), F32)],
        8,
        *(pos, pattern, coup, anc_rhs[0], yb),
        mib=UPPER_MIB,
    )
    near = add(keep0[0], got0[0])
    far = send_xor(add(keep0[1], got0[1]).astype(BF), 1).astype(F32)
    far, oth, right, left = lax.optimization_barrier((far, oth, right, left))
    got_layer = send_xor(send, 8)
    v = jnp.concatenate([jnp.where(flip, far, near), jnp.where(flip, near, far)]).astype(BF)

    def load_runs(name, *runs):
        count = sum(c for _, c in runs)
        kernel = functools.partial(runs_kernel, runs)
        outs = [((2, count, SEP, ANC), BF)]
        return call(kernel, name, "saa:v", outs, [], 2 * len(runs), pos, own, oth, cost=loading(count * 4))[0]

    def load_whole(name, index):
        kernel = functools.partial(whole_kernel, index)
        outs = [((ANC, ANC), BF)]
        return call(kernel, name, "s" + "a" * 10 + ":v", outs, [], 10, pos, own, oth, *around, cost=loading(16))[0]

    long = ((ANC, COLS), BF)
    zs = ring(v)
    got_core = send_xor(add(keep[:, 1], got_layer[:, 1]).astype(BF), 1)
    y0, pend, v = call(
        zeroth_kernel,
        "forward_level0",
        "svvvvvvvv:v",
        [((COLS, ROWS), BF), ((4, ROWS, COLS), F32), ((ROWS, COLS), BF)],
        [long],
        0,
        *(pos, load_runs("load_level0", (0, 5)), *zs, keep, got_layer, got_core),
    )
    v, right, left = lax.optimization_barrier((v, right, left))
    swapped = [send_xor(right, 1), send_xor(left, 1)]
    y1, mine, *pieces = call(
        first_kernel,
        "forward_level1",
        "svvvvvv:v",
        [((COLS, ROWS), BF), ((3, QUART, ROWS), F32)] + [((3, QUART, ROWS), BF)] * 3,
        [long, ((3, COLS, ROWS), F32)],
        0,
        *(pos, load_runs("load_level1", (5, 4)), *ring(v), pend),
    )
    middle = SEP // 2
    pieces, low, high, right, left, swapped = lax.optimization_barrier(
        (pieces, right[:, :middle], left[:, middle:], right, left, swapped)
    )
    low, high = send_ring(low, 1), send_ring(high, 3)
    got = [send_xor(pieces[m - 1], 16 * m) for m in (2, 3, 1)]
    pend = add(mine, *got)
    v = pend[:2].astype(BF)
    v, y1, low, high = lax.optimization_barrier((v, y1, low, high))
    around = [right, left, low, high] + swapped + [send_xor(low, 1), send_xor(high, 1)]
    thin, wide = ((QUART, ANC), BF), ((ANC, ANC), BF)
    blk23 = load_runs("load_levels23", (9, 1), (11, 3))
    y2, vy, v4 = call(
        middle_kernel,
        "forward_levels23",
        "s" + "a" * 10 + "v" * 6 + ":v",
        [((QUART, ROWS), BF), ((2, QUART, ROWS), BF), ((QUART, ROWS), BF)],
        [thin, thin, wide],
        10,
        *(pos, own, oth, *around, blk23, *ring(v), pend[2]),
    )
    got = send_xor(vy, 64)
    z4 = add(v4, got[0], send_xor(v4, 128), send_xor(v4, 192)).astype(BF)
    y3 = add(vy[1], got[1]).astype(BF)
    sol4, *outs = call(
        top_kernel,
        "top_levels",
        "svvvvvvvvv:v",
        [((QUART, ROWS), BF), ((2, QUART, ROWS), F32)] + [((2, QUART, ROWS), BF)] * 3,
        [thin, ((QUART, ANC), F32)],
        0,
        *(pos, blk23, load_whole("load_level4", 1), load_whole("load_level3", 0), *ring(z4), y2, y3),
    )
    sol23 = add(outs[0], *[send_ring(outs[d], d) for d in (2, 1, 3)])
    upper = jnp.concatenate([sol23.astype(BF), sol4[None]])
    y1 = add(y1, send_xor(y1, 16)).astype(BF)
    across = {m: send_xor(upper, 16 * m) for m in (1, 3, 2)}
    low0, low1 = load_runs("load_low0", (0, 1), (2, 3)), load_runs("load_low1", (5, 4))
    same, other, *outs = call(
        low_kernel,
        "low_levels",
        "s" + "v" * 9 + ":v",
        [((3, COLS, SEP), BF)] * 2 + [((2, COLS, ROWS), F32)] + [((2, COLS, ROWS), BF)] * 3,
        [((3, COLS, ROWS), BF), ((COLS, ANC), F32), ((COLS, 4 * SEP), BF)],
        0,
        *(pos, low0, low1, load_whole("load_low", 2), upper, *[across[m] for m in (1, 2, 3)], y0, y1),
    )
    sol01 = add(outs[0], *[send_ring(outs[d], d) for d in (2, 1, 3)])
    ups = [send_xor(other, 1), send_xor(same, 8), send_xor(other, 9)]
    lower, higher = sol01[..., :SEP].astype(BF), sol01[..., SEP:].astype(BF)
    home, away = jnp.where(flip, higher, lower), jnp.where(flip, lower, higher)
    got = [send_xor(away, 1), send_xor(home, 8), send_xor(away, 9)]
    rest, anc_up = call(
        rest_kernel,
        "leaf_rest",
        "ssvvvvvvv:v",
        [((1024, 512), F32), ((3, SEP, 512), F32)],
        [((3 * SEP, 512), BF), ((1024, 3 * SEP), BF)],
        0,
        *(pos, pattern, leaf_rhs, leaf_inv, coup, same, *ups),
    )
    x_leaf, x_anc = call(
        final_kernel,
        "leaf_backward",
        "ssvvvvvvvv:a",
        [((1024, 512), F32), ((LEVELS, SEP, 512), F32)],
        [((2 * SEP, 512), BF), ((1024, 2 * SEP), BF), ((1024, 512), F32), ((2, SEP, 512), F32)],
        11,
        *(pos, pattern, leaf_inv, coup, sol01, *got, rest, anc_up),
    )
    return x_leaf, x_anc[None]


def solution(mesh):
    placed = (
        P(("layer", "row"), None),
        P(("layer", "row"), None, None),
        P(("layer", "row"), None, None),
        P(("layer", "row"), None),
        P("layer", None, "row", None),
        P("layer", None, "row", None),
    )
    return jax.shard_map(
        body,
        mesh=mesh,
        in_specs=placed,
        out_specs=(P(("layer", "row"), None), P("layer", None, "row", None)),
        check_vma=False,
    )
```

```python
import functools

import jax
import jax.numpy as jnp
from jax import lax
from jax.experimental import pallas as pl
from jax.experimental.pallas import tpu as pltpu
from jax.sharding import PartitionSpec as P

BF = jnp.bfloat16
F32 = jnp.float32
LEVELS = 5
SUPERS = 8
SEP = 128
ROWS = 256
ANC = 1024
COLS = 128
QUART = 32
MIB = 24
UPPER_MIB = 58
LEAF_MIB = 58
CHIPS = 4
AXES = ("layer", "row")
PLACES = {
    "s": pl.BlockSpec(memory_space=pltpu.SMEM),
    "v": pl.BlockSpec(memory_space=pltpu.VMEM),
    "a": pl.BlockSpec(memory_space=pl.ANY),
}
WHOLE = (10, 14, 1)


def block_start(level):
    return level * LEVELS - level * (level - 1) // 2


def devices():
    return lax.axis_size("layer") * lax.axis_size("row")


def send_xor(value, mask):
    return lax.ppermute(value, AXES, [(i, i ^ mask) for i in range(devices())])


def send_ring(value, step):
    pairs = [(i, (i & ~6) | ((((i >> 1 & 3) + step) % CHIPS) << 1)) for i in range(devices())]
    return lax.ppermute(value, AXES, pairs)


def ring(value):
    got = {d: send_ring(value, d) for d in (1, 3, 2)}
    return [value] + [got[d] for d in (1, 2, 3)]


def part(start, size):
    return pl.ds(pl.multiple_of(start * size, size), size)


def dot(a, b):
    return jnp.dot(a, b, preferred_element_type=F32)


def dot_nt(a, b):
    return lax.dot_general(a, b, (((1,), (1,)), ((), ())), preferred_element_type=F32)


def dot_tn(a, b):
    return lax.dot_general(a, b, (((0,), (0,)), ((), ())), preferred_element_type=F32)


def start(pairs, sems):
    copies = [pltpu.make_async_copy(a, b, sems.at[i]) for i, (a, b) in enumerate(pairs)]
    for one in copies:
        one.start()
    return copies


def wait(copies):
    for one in copies:
        one.wait()


def runs_of(own, oth, runs, blk):
    pairs, at = [], 0
    for first, count in runs:
        for side, blocks in enumerate((own, oth)):
            pairs.append((blocks.at[pl.ds(first, count)], blk.at[side, pl.ds(at, count)]))
        at += count
    return pairs


def whole_of(index, own, oth, around, pos, target):
    chip, core = pos[0], pos[1]
    pairs = []
    for side, c in enumerate((core, 1 - core)):
        right, left, low, high = around[4 * side : 4 * side + 4]
        near = (own, oth)[side].at[WHOLE[index]]
        for source, d in ((near, 0), (right.at[index], 1), (left.at[index], 3)):
            row = 2 * ((chip + CHIPS - d) % CHIPS) + c
            pairs.append((source, target.at[part(row, SEP)]))
        row = 2 * (2 * ((chip + 2) % CHIPS) + c)
        pairs.append((low.at[index], target.at[part(row, SEP // 2)]))
        pairs.append((high.at[index], target.at[part(row + 1, SEP // 2)]))
    return pairs


def stack_of(blk, side, first, count):
    return blk[side, first : first + count].reshape(count * SEP, ANC)


def runs_kernel(runs, pos, own, oth, blk, sems):
    wait(start(runs_of(own, oth, runs, blk), sems))


def whole_kernel(index, pos, own, oth, *refs):
    around, whole, sems = refs[:8], refs[8], refs[9]
    wait(start(whole_of(index, own, oth, around, pos, whole), sems))


def masked_into(cm, coup, pattern, t):
    for k in range(SUPERS):
        rows = pl.ds(k * SEP, SEP)
        keep = pattern[k, t].astype(F32)
        cm[rows, :] = (coup[t, rows, :].astype(F32) * keep).astype(BF)


def split_share(share, group, keep, send):
    for m in range(2):
        keep[m] = share[:, part(group ^ m, COLS)]
        send[m] = share[:, part(group ^ (2 + m), COLS)].astype(BF)


def leaf_kernel(pos, pattern, rhs_in, inv_in, coup_in, anc_in, keep, send, yb, share, cm, rhs, inv, coup, anc, sems):
    pairs = [(inv_in, inv), (rhs_in, rhs), (coup_in.at[pl.ds(0, 1)], coup), (anc_in.at[0], anc)]
    copies = start(pairs, sems)
    wait(copies[:2])
    for k in range(SUPERS):
        rows = pl.ds(k * SEP, SEP)
        yb[rows, :] = dot(inv[k], rhs[rows, :]).astype(BF)
    wait(copies[2:])
    masked_into(cm, coup, pattern, 0)
    share[...] = anc[...] - dot_tn(cm[...], yb[...])
    split_share(share, pos[2], keep, send)


def upper_kernel(pos, pattern, coup_in, anc_in, yb, keep, send, share, cm, coup, anc, sems):
    pairs = []
    for t in range(1, LEVELS):
        pairs += [(coup_in.at[t], coup.at[t]), (anc_in.at[t], anc.at[t])]
    copies = start(pairs, sems)
    for t in range(1, LEVELS):
        wait(copies[2 * t - 2 : 2 * t])
        masked_into(cm, coup, pattern, t)
        share[...] = anc[t] - dot_tn(cm[...], yb[...])
        split_share(share, pos[2], keep.at[t - 1], send.at[t - 1])


def zeroth_kernel(pos, blk, z0, z1, z2, z3, keep, got_layer, got_core, y_out, pend, v_out, zabs):
    chip, core = pos[0], pos[1]
    for d, z in enumerate((z0, z1, z2, z3)):
        zabs[part((chip + CHIPS - d) % CHIPS, ROWS), :] = z[...]
    for side, half in enumerate((core, 1 - core)):
        product = dot(stack_of(blk, side, 0, 5), zabs[...])
        y_out[:, part(half, SEP)] = product[:SEP].T.astype(BF)
        for k in range(4):
            if side == 0:
                base = keep[k, 0] + got_layer[k, 0].astype(F32)
            else:
                base = got_core[k].astype(F32)
            after = base - product[(k + 1) * SEP : (k + 2) * SEP]
            pend[k, part(half, SEP), :] = after
            if k == 0:
                v_out[part(half, SEP), :] = after.astype(BF)


def first_kernel(pos, blk, z0, z1, z2, z3, pend, y_out, mine, s1, s2, s3, zabs, turned):
    chip, core, quart = pos[0], pos[1], pos[3]
    for d, z in enumerate((z0, z1, z2, z3)):
        zabs[part((chip + CHIPS - d) % CHIPS, ROWS), :] = z[...]
    for side, half in enumerate((core, 1 - core)):
        product = dot(stack_of(blk, side, 0, 4), zabs[...])
        y_out[:, part(half, SEP)] = product[:SEP].T.astype(BF)
        for k in range(3):
            after = pend[k + 1, part(half, SEP), :] - product[(k + 1) * SEP : (k + 2) * SEP]
            turned[k, :, part(half, SEP)] = after.T
    for m, out in enumerate((mine, s1, s2, s3)):
        for k in range(3):
            out[k] = turned[k, part(quart ^ m, QUART), :].astype(out.dtype)


def middle_kernel(pos, own, oth, *refs):
    around, (blk, z0, z1, z2, z3, pend, y2, vy, v4), refs = refs[:8], refs[8:17], refs[17:]
    za, zb, whole, sems = refs
    copies = start(whole_of(0, own, oth, around, pos, whole), sems)
    chip, core = pos[0], pos[1]
    for d, z in enumerate((z0, z1, z2, z3)):
        place = part((chip + CHIPS - d) % CHIPS, ROWS)
        za[:, place] = z[0]
        zb[:, place] = z[1]
    wait(copies)
    zb[...] = (zb[...].astype(F32) - dot_nt(za[...], whole[...])).astype(BF)
    for side, half in enumerate((core, 1 - core)):
        two = dot_nt(za[...], stack_of(blk, side, 0, 2))
        three = dot_nt(zb[...], stack_of(blk, side, 2, 2))
        y2[:, part(half, SEP)] = two[:, :SEP].astype(BF)
        vy[1, :, part(half, SEP)] = three[:, :SEP].astype(BF)
        after = (pend[:, part(half, SEP)] - two[:, SEP:] - three[:, SEP:]).astype(BF)
        vy[0, :, part(half, SEP)] = after
        v4[:, part(half, SEP)] = after


def hand_out(total, level_at, chip, outs):
    for d, out in enumerate(outs):
        out[level_at] = total[:, part((chip + d) % CHIPS, ROWS)].astype(out.dtype)


def top_kernel(pos, blk, whole4, whole3, z0, z1, z2, z3, y2, y3, solb, *refs):
    outs, (za, total) = refs[:4], refs[4:]
    chip, core = pos[0], pos[1]
    for d, z in enumerate((z0, z1, z2, z3)):
        za[:, part((chip + CHIPS - d) % CHIPS, ROWS)] = z[...]
    y4 = dot_nt(za[...], whole4[...]).astype(BF)
    solb[...] = dot(y4, whole4[:, part(chip, ROWS)]).astype(BF)
    third = second = None
    for side, half in enumerate((core, 1 - core)):
        minus = -solb[:, part(half, SEP)]
        one = dot(jnp.concatenate([y3[:, part(half, SEP)], minus], axis=1), stack_of(blk, side, 2, 2))
        two = dot(jnp.concatenate([y2[:, part(half, SEP)], minus], axis=1), stack_of(blk, side, 0, 2))
        third = one if third is None else third + one
        second = two if second is None else second + two
    total[...] = third
    hand_out(total, 1, chip, outs)
    total[...] = second - dot(third.astype(BF), whole3[...])
    hand_out(total, 0, chip, outs)


def low_kernel(pos, blk0, blk1, whole, u0, u1, u2, u3, y0, y1, same, other, *refs):
    outs, (solb, total, vals) = refs[:4], refs[4:]
    chip, core, quart = pos[0], pos[1], pos[3]
    for m, piece in enumerate((u0, u1, u2, u3)):
        for k in range(3):
            solb[k, part(quart ^ m, QUART), :] = piece[k]
    same[...] = solb[:, :, part(core, SEP)]
    other[...] = solb[:, :, part(1 - core, SEP)]
    first = zeroth = None
    for side, half in enumerate((core, 1 - core)):
        vals[:, 0:SEP] = y1[:, part(half, SEP)]
        for k in range(3):
            vals[:, SEP * (k + 1) : SEP * (k + 2)] = -solb[k, :, part(half, SEP)]
        one = dot(vals[...], stack_of(blk1, side, 0, 4))
        both = jnp.concatenate([y0[:, part(half, SEP)], vals[:, SEP:]], axis=1)
        two = dot(both, stack_of(blk0, side, 0, 4))
        first = one if first is None else first + one
        zeroth = two if zeroth is None else zeroth + two
    total[...] = first
    hand_out(total, 1, chip, outs)
    total[...] = zeroth - dot(first.astype(BF), whole[...])
    hand_out(total, 0, chip, outs)


def spread(x_anc, t, group, first, others):
    x_anc[t, :, part(group, COLS)] = first.T
    for m in range(1, 4):
        x_anc[t, :, part(group ^ m, COLS)] = others[m - 1].astype(F32).T


def rest_kernel(pos, pattern, rhs, inv, coup, upper, up1, up2, up3, rest, x_anc, solved, cm):
    for t in range(3):
        spread(x_anc, t, pos[2], upper[t].astype(F32), (up1[t], up2[t], up3[t]))
        solved[t * SEP : (t + 1) * SEP, :] = x_anc[t].astype(BF)
        masked_into(cm.at[:, pl.ds(t * SEP, SEP)], coup, pattern, t + 2)
    for k in range(SUPERS):
        rows = pl.ds(k * SEP, SEP)
        rest[rows, :] = dot(inv[k], rhs[rows, :]) - dot(cm[rows, :], solved[...])


def final_kernel(pos, pattern, inv, coup, sol01, got1, got2, got3, rest, anc_up, *refs):
    leaf_out, anc_out, solved, cm, x_leaf, x_anc, sems = refs
    copies = []

    def put(source, target):
        one = pltpu.make_async_copy(source, target, sems.at[len(copies)])
        one.start()
        copies.append(one)

    put(anc_up, anc_out.at[pl.ds(2, 3)])
    for t in range(2):
        first = sol01[t, :, part(pos[1], SEP)]
        spread(x_anc, t, pos[2], first, (got1[t], got2[t], got3[t]))
        put(x_anc.at[t], anc_out.at[t])
        solved[t * SEP : (t + 1) * SEP, :] = x_anc[t].astype(BF)
    for t in range(2):
        masked_into(cm.at[:, pl.ds(t * SEP, SEP)], coup, pattern, t)
    for k in range(SUPERS):
        rows = pl.ds(k * SEP, SEP)
        leaf_vb = (rest[rows, :] - dot(cm[rows, :], solved[...])).astype(BF)
        x_leaf[rows, :] = dot_tn(inv[k], leaf_vb)
        put(x_leaf.at[rows], leaf_out.at[rows])
    wait(copies)


def call(kernel, name, places, outs, scratch, sems, *args, mib=MIB, cost=None):
    shapes = [jax.ShapeDtypeStruct(dims, dtype) for dims, dtype in outs]
    scratch = [pltpu.VMEM(dims, dtype) for dims, dtype in scratch]
    if sems:
        scratch.append(pltpu.SemaphoreType.DMA((sems,)))
    here, there = places.split(":")
    return pl.pallas_call(
        kernel,
        out_shape=shapes,
        in_specs=[PLACES[p] for p in here],
        out_specs=[PLACES[there]] * len(outs),
        scratch_shapes=scratch,
        compiler_params=pltpu.CompilerParams(vmem_limit_bytes=mib * 1024 * 1024),
        cost_estimate=cost,
        name=name,
    )(*args)


def loading(parts):
    return pl.CostEstimate(flops=1, bytes_accessed=parts * SEP * ANC * 2, transcendentals=0)


def add(*values):
    return functools.reduce(jnp.add, [v.astype(F32) for v in values])


def body(leaf_rhs, leaf_inv, coupling, pattern, anc_rhs, anc_blocks):
    layer, row = lax.axis_index("layer"), lax.axis_index("row")
    chip, core = row // 2, row % 2
    flip = core == 1
    pos = jnp.stack([chip, core, (layer % 2) * 2 + core, layer // 2 % 4]).astype(jnp.int32)
    coup = coupling.transpose(1, 0, 2)
    own = anc_blocks[0]

    chosen = jnp.stack([own[k] for k in WHOLE])
    pos, chosen = lax.optimization_barrier((pos, chosen))
    oth = send_xor(own, 1)
    right, left = send_ring(chosen, 1), send_ring(chosen, 3)

    keep0, send0, yb = call(
        leaf_kernel,
        "leaf_forward",
        "ssaaaa:v",
        [((2, SEP, COLS), F32), ((2, SEP, COLS), BF), ((1024, 512), BF)],
        [((SEP, 512), F32), ((1024, SEP), BF), ((1024, 512), BF), ((SUPERS, SEP, SEP), BF)]
        + [((1, 1024, SEP), BF), ((SEP, 512), F32)],
        4,
        *(pos, pattern, leaf_rhs, leaf_inv, coup, anc_rhs[0]),
        mib=LEAF_MIB,
    )
    got0 = send_xor(send0, 8)
    keep, send = call(
        upper_kernel,
        "leaf_upper",
        "ssaav:v",
        [((4, 2, SEP, COLS), F32), ((4, 2, SEP, COLS), BF)],
        [((SEP, 512), F32), ((1024, SEP), BF), ((LEVELS, 1024, SEP), BF), ((LEVELS, SEP, 512), F32)],
        8,
        *(pos, pattern, coup, anc_rhs[0], yb),
        mib=UPPER_MIB,
    )
    near = add(keep0[0], got0[0])
    far = send_xor(add(keep0[1], got0[1]).astype(BF), 1).astype(F32)
    far, oth, right, left = lax.optimization_barrier((far, oth, right, left))
    got_layer = send_xor(send, 8)
    v = jnp.concatenate([jnp.where(flip, far, near), jnp.where(flip, near, far)]).astype(BF)

    def load_runs(name, *runs):
        count = sum(c for _, c in runs)
        kernel = functools.partial(runs_kernel, runs)
        outs = [((2, count, SEP, ANC), BF)]
        return call(kernel, name, "saa:v", outs, [], 2 * len(runs), pos, own, oth, cost=loading(count * 4))[0]

    def load_whole(name, index):
        kernel = functools.partial(whole_kernel, index)
        outs = [((ANC, ANC), BF)]
        return call(kernel, name, "s" + "a" * 10 + ":v", outs, [], 10, pos, own, oth, *around, cost=loading(16))[0]

    long = ((ANC, COLS), BF)
    zs = ring(v)
    got_core = send_xor(add(keep[:, 1], got_layer[:, 1]).astype(BF), 1)
    y0, pend, v = call(
        zeroth_kernel,
        "forward_level0",
        "svvvvvvvv:v",
        [((COLS, ROWS), BF), ((4, ROWS, COLS), F32), ((ROWS, COLS), BF)],
        [long],
        0,
        *(pos, load_runs("load_level0", (0, 5)), *zs, keep, got_layer, got_core),
    )
    v, right, left = lax.optimization_barrier((v, right, left))
    swapped = [send_xor(right, 1), send_xor(left, 1)]
    y1, mine, *pieces = call(
        first_kernel,
        "forward_level1",
        "svvvvvv:v",
        [((COLS, ROWS), BF), ((3, QUART, ROWS), F32)] + [((3, QUART, ROWS), BF)] * 3,
        [long, ((3, COLS, ROWS), F32)],
        0,
        *(pos, load_runs("load_level1", (5, 4)), *ring(v), pend),
    )
    middle = SEP // 2
    pieces, low, high, right, left, swapped = lax.optimization_barrier(
        (pieces, right[:, :middle], left[:, middle:], right, left, swapped)
    )
    low, high = send_ring(low, 1), send_ring(high, 3)
    got = [send_xor(pieces[m - 1], 16 * m) for m in (2, 3, 1)]
    pend = add(mine, *got)
    v = pend[:2].astype(BF)
    v, y1, low, high = lax.optimization_barrier((v, y1, low, high))
    around = [right, left, low, high] + swapped + [send_xor(low, 1), send_xor(high, 1)]
    thin, wide = ((QUART, ANC), BF), ((ANC, ANC), BF)
    blk23 = load_runs("load_levels23", (9, 1), (11, 3))
    y2, vy, v4 = call(
        middle_kernel,
        "forward_levels23",
        "s" + "a" * 10 + "v" * 6 + ":v",
        [((QUART, ROWS), BF), ((2, QUART, ROWS), BF), ((QUART, ROWS), BF)],
        [thin, thin, wide],
        10,
        *(pos, own, oth, *around, blk23, *ring(v), pend[2]),
    )
    got = send_xor(vy, 64)
    z4 = add(v4, got[0], send_xor(v4, 128), send_xor(v4, 192)).astype(BF)
    y3 = add(vy[1], got[1]).astype(BF)
    sol4, *outs = call(
        top_kernel,
        "top_levels",
        "svvvvvvvvv:v",
        [((QUART, ROWS), BF), ((2, QUART, ROWS), F32)] + [((2, QUART, ROWS), BF)] * 3,
        [thin, ((QUART, ANC), F32)],
        0,
        *(pos, blk23, load_whole("load_level4", 1), load_whole("load_level3", 0), *ring(z4), y2, y3),
    )
    sol23 = add(outs[0], *[send_ring(outs[d], d) for d in (2, 1, 3)])
    upper = jnp.concatenate([sol23.astype(BF), sol4[None]])
    y1 = add(y1, send_xor(y1, 16)).astype(BF)
    across = {m: send_xor(upper, 16 * m) for m in (1, 3, 2)}
    low0, low1 = load_runs("load_low0", (0, 1), (2, 3)), load_runs("load_low1", (5, 4))
    same, other, *outs = call(
        low_kernel,
        "low_levels",
        "s" + "v" * 9 + ":v",
        [((3, COLS, SEP), BF)] * 2 + [((2, COLS, ROWS), F32)] + [((2, COLS, ROWS), BF)] * 3,
        [((3, COLS, ROWS), BF), ((COLS, ANC), F32), ((COLS, 4 * SEP), BF)],
        0,
        *(pos, low0, low1, load_whole("load_low", 2), upper, *[across[m] for m in (1, 2, 3)], y0, y1),
    )
    sol01 = add(outs[0], *[send_ring(outs[d], d) for d in (2, 1, 3)])
    ups = [send_xor(other, 1), send_xor(same, 8), send_xor(other, 9)]
    lower, higher = sol01[..., :SEP].astype(BF), sol01[..., SEP:].astype(BF)
    home, away = jnp.where(flip, higher, lower), jnp.where(flip, lower, higher)
    got = [send_xor(away, 1), send_xor(home, 8), send_xor(away, 9)]
    rest, anc_up = call(
        rest_kernel,
        "leaf_rest",
        "ssvvvvvvv:v",
        [((1024, 512), F32), ((3, SEP, 512), F32)],
        [((3 * SEP, 512), BF), ((1024, 3 * SEP), BF)],
        0,
        *(pos, pattern, leaf_rhs, leaf_inv, coup, same, *ups),
    )
    x_leaf, x_anc = call(
        final_kernel,
        "leaf_backward",
        "ssvvvvvvvv:a",
        [((1024, 512), F32), ((LEVELS, SEP, 512), F32)],
        [((2 * SEP, 512), BF), ((1024, 2 * SEP), BF), ((1024, 512), F32), ((2, SEP, 512), F32)],
        11,
        *(pos, pattern, leaf_inv, coup, sol01, *got, rest, anc_up),
    )
    return x_leaf, x_anc[None]


def solution(mesh):
    placed = (
        P(("layer", "row"), None),
        P(("layer", "row"), None, None),
        P(("layer", "row"), None, None),
        P(("layer", "row"), None),
        P("layer", None, "row", None),
        P("layer", None, "row", None),
    )
    return jax.shard_map(
        body,
        mesh=mesh,
        in_specs=placed,
        out_specs=(P(("layer", "row"), None), P("layer", None, "row", None)),
        check_vma=False,
    )
```

```python
import functools

import jax
import jax.numpy as jnp
from jax import lax
from jax.experimental import pallas as pl
from jax.experimental.pallas import tpu as pltpu
from jax.sharding import PartitionSpec as P

BF = jnp.bfloat16
F32 = jnp.float32
LEVELS = 5
SUPERS = 8
SEP = 128
ROWS = 256
ANC = 1024
COLS = 128
QUART = 32
MIB = 24
UPPER_MIB = 58
LEAF_MIB = 58
CHIPS = 4
AXES = ("layer", "row")
PLACES = {
    "s": pl.BlockSpec(memory_space=pltpu.SMEM),
    "v": pl.BlockSpec(memory_space=pltpu.VMEM),
    "a": pl.BlockSpec(memory_space=pl.ANY),
}
WHOLE = (10, 14, 1)


def block_start(level):
    return level * LEVELS - level * (level - 1) // 2


def devices():
    return lax.axis_size("layer") * lax.axis_size("row")


def send_xor(value, mask):
    return lax.ppermute(value, AXES, [(i, i ^ mask) for i in range(devices())])


def send_ring(value, step):
    pairs = [(i, (i & ~6) | ((((i >> 1 & 3) + step) % CHIPS) << 1)) for i in range(devices())]
    return lax.ppermute(value, AXES, pairs)


def ring(value):
    got = {d: send_ring(value, d) for d in (1, 3, 2)}
    return [value] + [got[d] for d in (1, 2, 3)]


def part(start, size):
    return pl.ds(pl.multiple_of(start * size, size), size)


def dot(a, b):
    return jnp.dot(a, b, preferred_element_type=F32)


def dot_nt(a, b):
    return lax.dot_general(a, b, (((1,), (1,)), ((), ())), preferred_element_type=F32)


def dot_tn(a, b):
    return lax.dot_general(a, b, (((0,), (0,)), ((), ())), preferred_element_type=F32)


def start(pairs, sems):
    copies = [pltpu.make_async_copy(a, b, sems.at[i]) for i, (a, b) in enumerate(pairs)]
    for one in copies:
        one.start()
    return copies


def wait(copies):
    for one in copies:
        one.wait()


def runs_of(own, oth, runs, blk):
    pairs, at = [], 0
    for first, count in runs:
        for side, blocks in enumerate((own, oth)):
            pairs.append((blocks.at[pl.ds(first, count)], blk.at[side, pl.ds(at, count)]))
        at += count
    return pairs


def whole_of(index, own, oth, around, pos, target):
    chip, core = pos[0], pos[1]
    pairs = []
    for side, c in enumerate((core, 1 - core)):
        right, left, low, high = around[4 * side : 4 * side + 4]
        near = (own, oth)[side].at[WHOLE[index]]
        for source, d in ((near, 0), (right.at[index], 1), (left.at[index], 3)):
            row = 2 * ((chip + CHIPS - d) % CHIPS) + c
            pairs.append((source, target.at[part(row, SEP)]))
        row = 2 * (2 * ((chip + 2) % CHIPS) + c)
        pairs.append((low.at[index], target.at[part(row, SEP // 2)]))
        pairs.append((high.at[index], target.at[part(row + 1, SEP // 2)]))
    return pairs


def stack_of(blk, side, first, count):
    return blk[side, first : first + count].reshape(count * SEP, ANC)


def runs_kernel(runs, pos, own, oth, blk, sems):
    wait(start(runs_of(own, oth, runs, blk), sems))


def whole_kernel(index, pos, own, oth, *refs):
    around, whole, sems = refs[:8], refs[8], refs[9]
    wait(start(whole_of(index, own, oth, around, pos, whole), sems))


def masked_into(cm, coup, pattern, t):
    for k in range(SUPERS):
        rows = pl.ds(k * SEP, SEP)
        keep = pattern[k, t].astype(F32)
        cm[rows, :] = (coup[t, rows, :].astype(F32) * keep).astype(BF)


def split_share(share, group, keep, send):
    for m in range(2):
        keep[m] = share[:, part(group ^ m, COLS)]
        send[m] = share[:, part(group ^ (2 + m), COLS)].astype(BF)


def leaf_kernel(pos, pattern, rhs_in, inv_in, coup_in, anc_in, keep, send, yb, share, cm, rhs, inv, coup, anc, sems):
    pairs = [(inv_in, inv), (rhs_in, rhs), (coup_in.at[pl.ds(0, 1)], coup), (anc_in.at[0], anc)]
    copies = start(pairs, sems)
    wait(copies[:2])
    for k in range(SUPERS):
        rows = pl.ds(k * SEP, SEP)
        yb[rows, :] = dot(inv[k], rhs[rows, :]).astype(BF)
    wait(copies[2:])
    masked_into(cm, coup, pattern, 0)
    share[...] = anc[...] - dot_tn(cm[...], yb[...])
    split_share(share, pos[2], keep, send)


def upper_kernel(pos, pattern, coup_in, anc_in, yb, keep, send, share, cm, coup, anc, sems):
    pairs = []
    for t in range(1, LEVELS):
        pairs += [(coup_in.at[t], coup.at[t]), (anc_in.at[t], anc.at[t])]
    copies = start(pairs, sems)
    for t in range(1, LEVELS):
        wait(copies[2 * t - 2 : 2 * t])
        masked_into(cm, coup, pattern, t)
        share[...] = anc[t] - dot_tn(cm[...], yb[...])
        split_share(share, pos[2], keep.at[t - 1], send.at[t - 1])


def zeroth_kernel(pos, blk, z0, z1, z2, z3, keep, got_layer, got_core, y_out, pend, v_out, zabs):
    chip, core = pos[0], pos[1]
    for d, z in enumerate((z0, z1, z2, z3)):
        zabs[part((chip + CHIPS - d) % CHIPS, ROWS), :] = z[...]
    for side, half in enumerate((core, 1 - core)):
        product = dot(stack_of(blk, side, 0, 5), zabs[...])
        y_out[:, part(half, SEP)] = product[:SEP].T.astype(BF)
        for k in range(4):
            if side == 0:
                base = keep[k, 0] + got_layer[k, 0].astype(F32)
            else:
                base = got_core[k].astype(F32)
            after = base - product[(k + 1) * SEP : (k + 2) * SEP]
            pend[k, part(half, SEP), :] = after
            if k == 0:
                v_out[part(half, SEP), :] = after.astype(BF)


def first_kernel(pos, blk, z0, z1, z2, z3, pend, y_out, mine, s1, s2, s3, zabs, turned):
    chip, core, quart = pos[0], pos[1], pos[3]
    for d, z in enumerate((z0, z1, z2, z3)):
        zabs[part((chip + CHIPS - d) % CHIPS, ROWS), :] = z[...]
    for side, half in enumerate((core, 1 - core)):
        product = dot(stack_of(blk, side, 0, 4), zabs[...])
        y_out[:, part(half, SEP)] = product[:SEP].T.astype(BF)
        for k in range(3):
            after = pend[k + 1, part(half, SEP), :] - product[(k + 1) * SEP : (k + 2) * SEP]
            turned[k, :, part(half, SEP)] = after.T
    for m, out in enumerate((mine, s1, s2, s3)):
        for k in range(3):
            out[k] = turned[k, part(quart ^ m, QUART), :].astype(out.dtype)


def middle_kernel(pos, own, oth, *refs):
    around, (blk, z0, z1, z2, z3, pend, y2, vy, v4), refs = refs[:8], refs[8:17], refs[17:]
    za, zb, whole, sems = refs
    copies = start(whole_of(0, own, oth, around, pos, whole), sems)
    chip, core = pos[0], pos[1]
    for d, z in enumerate((z0, z1, z2, z3)):
        place = part((chip + CHIPS - d) % CHIPS, ROWS)
        za[:, place] = z[0]
        zb[:, place] = z[1]
    wait(copies)
    zb[...] = (zb[...].astype(F32) - dot_nt(za[...], whole[...])).astype(BF)
    for side, half in enumerate((core, 1 - core)):
        two = dot_nt(za[...], stack_of(blk, side, 0, 2))
        three = dot_nt(zb[...], stack_of(blk, side, 2, 2))
        y2[:, part(half, SEP)] = two[:, :SEP].astype(BF)
        vy[1, :, part(half, SEP)] = three[:, :SEP].astype(BF)
        after = (pend[:, part(half, SEP)] - two[:, SEP:] - three[:, SEP:]).astype(BF)
        vy[0, :, part(half, SEP)] = after
        v4[:, part(half, SEP)] = after


def hand_out(total, level_at, chip, outs):
    for d, out in enumerate(outs):
        out[level_at] = total[:, part((chip + d) % CHIPS, ROWS)].astype(out.dtype)


def top_kernel(pos, blk, whole4, whole3, z0, z1, z2, z3, y2, y3, solb, *refs):
    outs, (za, total) = refs[:4], refs[4:]
    chip, core = pos[0], pos[1]
    for d, z in enumerate((z0, z1, z2, z3)):
        za[:, part((chip + CHIPS - d) % CHIPS, ROWS)] = z[...]
    y4 = dot_nt(za[...], whole4[...]).astype(BF)
    solb[...] = dot(y4, whole4[:, part(chip, ROWS)]).astype(BF)
    third = second = None
    for side, half in enumerate((core, 1 - core)):
        minus = -solb[:, part(half, SEP)]
        one = dot(jnp.concatenate([y3[:, part(half, SEP)], minus], axis=1), stack_of(blk, side, 2, 2))
        two = dot(jnp.concatenate([y2[:, part(half, SEP)], minus], axis=1), stack_of(blk, side, 0, 2))
        third = one if third is None else third + one
        second = two if second is None else second + two
    total[...] = third
    hand_out(total, 1, chip, outs)
    total[...] = second - dot(third.astype(BF), whole3[...])
    hand_out(total, 0, chip, outs)


def low_kernel(pos, blk0, blk1, whole, u0, u1, u2, u3, y0, y1, same, other, *refs):
    outs, (solb, total, vals) = refs[:4], refs[4:]
    chip, core, quart = pos[0], pos[1], pos[3]
    for m, piece in enumerate((u0, u1, u2, u3)):
        for k in range(3):
            solb[k, part(quart ^ m, QUART), :] = piece[k]
    same[...] = solb[:, :, part(core, SEP)]
    other[...] = solb[:, :, part(1 - core, SEP)]
    first = zeroth = None
    for side, half in enumerate((core, 1 - core)):
        vals[:, 0:SEP] = y1[:, part(half, SEP)]
        for k in range(3):
            vals[:, SEP * (k + 1) : SEP * (k + 2)] = -solb[k, :, part(half, SEP)]
        one = dot(vals[...], stack_of(blk1, side, 0, 4))
        both = jnp.concatenate([y0[:, part(half, SEP)], vals[:, SEP:]], axis=1)
        two = dot(both, stack_of(blk0, side, 0, 4))
        first = one if first is None else first + one
        zeroth = two if zeroth is None else zeroth + two
    total[...] = first
    hand_out(total, 1, chip, outs)
    total[...] = zeroth - dot(first.astype(BF), whole[...])
    hand_out(total, 0, chip, outs)


def spread(x_anc, t, group, first, others):
    x_anc[t, :, part(group, COLS)] = first.T
    for m in range(1, 4):
        x_anc[t, :, part(group ^ m, COLS)] = others[m - 1].astype(F32).T


def rest_kernel(pos, pattern, rhs, inv, coup, upper, up1, up2, up3, rest, x_anc, solved, cm):
    for t in range(3):
        spread(x_anc, t, pos[2], upper[t].astype(F32), (up1[t], up2[t], up3[t]))
        solved[t * SEP : (t + 1) * SEP, :] = x_anc[t].astype(BF)
        masked_into(cm.at[:, pl.ds(t * SEP, SEP)], coup, pattern, t + 2)
    for k in range(SUPERS):
        rows = pl.ds(k * SEP, SEP)
        rest[rows, :] = dot(inv[k], rhs[rows, :]) - dot(cm[rows, :], solved[...])


def final_kernel(pos, pattern, inv, coup, sol01, got1, got2, got3, rest, anc_up, *refs):
    leaf_out, anc_out, solved, cm, x_leaf, x_anc, sems = refs
    copies = []

    def put(source, target):
        one = pltpu.make_async_copy(source, target, sems.at[len(copies)])
        one.start()
        copies.append(one)

    put(anc_up, anc_out.at[pl.ds(2, 3)])
    for t in range(2):
        first = sol01[t, :, part(pos[1], SEP)]
        spread(x_anc, t, pos[2], first, (got1[t], got2[t], got3[t]))
        put(x_anc.at[t], anc_out.at[t])
        solved[t * SEP : (t + 1) * SEP, :] = x_anc[t].astype(BF)
    for t in range(2):
        masked_into(cm.at[:, pl.ds(t * SEP, SEP)], coup, pattern, t)
    for k in range(SUPERS):
        rows = pl.ds(k * SEP, SEP)
        leaf_vb = (rest[rows, :] - dot(cm[rows, :], solved[...])).astype(BF)
        x_leaf[rows, :] = dot_tn(inv[k], leaf_vb)
        put(x_leaf.at[rows], leaf_out.at[rows])
    wait(copies)


def call(kernel, name, places, outs, scratch, sems, *args, mib=MIB, cost=None):
    shapes = [jax.ShapeDtypeStruct(dims, dtype) for dims, dtype in outs]
    scratch = [pltpu.VMEM(dims, dtype) for dims, dtype in scratch]
    if sems:
        scratch.append(pltpu.SemaphoreType.DMA((sems,)))
    here, there = places.split(":")
    return pl.pallas_call(
        kernel,
        out_shape=shapes,
        in_specs=[PLACES[p] for p in here],
        out_specs=[PLACES[there]] * len(outs),
        scratch_shapes=scratch,
        compiler_params=pltpu.CompilerParams(vmem_limit_bytes=mib * 1024 * 1024),
        cost_estimate=cost,
        name=name,
    )(*args)


def loading(parts):
    return pl.CostEstimate(flops=1, bytes_accessed=parts * SEP * ANC * 2, transcendentals=0)


def add(*values):
    return functools.reduce(jnp.add, [v.astype(F32) for v in values])


def body(leaf_rhs, leaf_inv, coupling, pattern, anc_rhs, anc_blocks):
    layer, row = lax.axis_index("layer"), lax.axis_index("row")
    chip, core = row // 2, row % 2
    flip = core == 1
    pos = jnp.stack([chip, core, (layer % 2) * 2 + core, layer // 2 % 4]).astype(jnp.int32)
    coup = coupling.transpose(1, 0, 2)
    own = anc_blocks[0]

    chosen = jnp.stack([own[k] for k in WHOLE])
    pos, chosen = lax.optimization_barrier((pos, chosen))
    oth = send_xor(own, 1)
    right, left = send_ring(chosen, 1), send_ring(chosen, 3)

    keep0, send0, yb = call(
        leaf_kernel,
        "leaf_forward",
        "ssaaaa:v",
        [((2, SEP, COLS), F32), ((2, SEP, COLS), BF), ((1024, 512), BF)],
        [((SEP, 512), F32), ((1024, SEP), BF), ((1024, 512), BF), ((SUPERS, SEP, SEP), BF)]
        + [((1, 1024, SEP), BF), ((SEP, 512), F32)],
        4,
        *(pos, pattern, leaf_rhs, leaf_inv, coup, anc_rhs[0]),
        mib=LEAF_MIB,
    )
    got0 = send_xor(send0, 8)
    keep, send = call(
        upper_kernel,
        "leaf_upper",
        "ssaav:v",
        [((4, 2, SEP, COLS), F32), ((4, 2, SEP, COLS), BF)],
        [((SEP, 512), F32), ((1024, SEP), BF), ((LEVELS, 1024, SEP), BF), ((LEVELS, SEP, 512), F32)],
        8,
        *(pos, pattern, coup, anc_rhs[0], yb),
        mib=UPPER_MIB,
    )
    near = add(keep0[0], got0[0])
    far = send_xor(add(keep0[1], got0[1]).astype(BF), 1).astype(F32)
    far, oth, right, left = lax.optimization_barrier((far, oth, right, left))
    got_layer = send_xor(send, 8)
    v = jnp.concatenate([jnp.where(flip, far, near), jnp.where(flip, near, far)]).astype(BF)

    def load_runs(name, *runs):
        count = sum(c for _, c in runs)
        kernel = functools.partial(runs_kernel, runs)
        outs = [((2, count, SEP, ANC), BF)]
        return call(kernel, name, "saa:v", outs, [], 2 * len(runs), pos, own, oth, cost=loading(count * 4), mib=48)[0]

    def load_whole(name, index):
        kernel = functools.partial(whole_kernel, index)
        outs = [((ANC, ANC), BF)]
        return call(kernel, name, "s" + "a" * 10 + ":v", outs, [], 10, pos, own, oth, *around, cost=loading(16))[0]

    long = ((ANC, COLS), BF)
    zs = ring(v)
    got_core = send_xor(add(keep[:, 1], got_layer[:, 1]).astype(BF), 1)
    y0, pend, v = call(
        zeroth_kernel,
        "forward_level0",
        "svvvvvvvv:v",
        [((COLS, ROWS), BF), ((4, ROWS, COLS), F32), ((ROWS, COLS), BF)],
        [long],
        0,
        *(pos, load_runs("load_level0", (0, 5)), *zs, keep, got_layer, got_core),
    )
    v, right, left = lax.optimization_barrier((v, right, left))
    swapped = [send_xor(right, 1), send_xor(left, 1)]
    y1, mine, *pieces = call(
        first_kernel,
        "forward_level1",
        "svvvvvv:v",
        [((COLS, ROWS), BF), ((3, QUART, ROWS), F32)] + [((3, QUART, ROWS), BF)] * 3,
        [long, ((3, COLS, ROWS), F32)],
        0,
        *(pos, load_runs("load_level1", (5, 4)), *ring(v), pend),
    )
    middle = SEP // 2
    pieces, low, high, right, left, swapped = lax.optimization_barrier(
        (pieces, right[:, :middle], left[:, middle:], right, left, swapped)
    )
    low, high = send_ring(low, 1), send_ring(high, 3)
    got = [send_xor(pieces[m - 1], 16 * m) for m in (2, 3, 1)]
    pend = add(mine, *got)
    v = pend[:2].astype(BF)
    v, y1, low, high = lax.optimization_barrier((v, y1, low, high))
    around = [right, left, low, high] + swapped + [send_xor(low, 1), send_xor(high, 1)]
    thin, wide = ((QUART, ANC), BF), ((ANC, ANC), BF)
    blk23 = load_runs("load_levels23", (9, 1), (11, 3))
    y2, vy, v4 = call(
        middle_kernel,
        "forward_levels23",
        "s" + "a" * 10 + "v" * 6 + ":v",
        [((QUART, ROWS), BF), ((2, QUART, ROWS), BF), ((QUART, ROWS), BF)],
        [thin, thin, wide],
        10,
        *(pos, own, oth, *around, blk23, *ring(v), pend[2]),
    )
    got = send_xor(vy, 64)
    z4 = add(v4, got[0], send_xor(v4, 128), send_xor(v4, 192)).astype(BF)
    y3 = add(vy[1], got[1]).astype(BF)
    sol4, *outs = call(
        top_kernel,
        "top_levels",
        "svvvvvvvvv:v",
        [((QUART, ROWS), BF), ((2, QUART, ROWS), F32)] + [((2, QUART, ROWS), BF)] * 3,
        [thin, ((QUART, ANC), F32)],
        0,
        *(pos, blk23, load_whole("load_level4", 1), load_whole("load_level3", 0), *ring(z4), y2, y3),
    )
    sol23 = add(outs[0], *[send_ring(outs[d], d) for d in (2, 1, 3)])
    upper = jnp.concatenate([sol23.astype(BF), sol4[None]])
    y1 = add(y1, send_xor(y1, 16)).astype(BF)
    across = {m: send_xor(upper, 16 * m) for m in (1, 3, 2)}
    low0, low1 = load_runs("load_low0", (0, 1), (2, 3)), load_runs("load_low1", (5, 4))
    same, other, *outs = call(
        low_kernel,
        "low_levels",
        "s" + "v" * 9 + ":v",
        [((3, COLS, SEP), BF)] * 2 + [((2, COLS, ROWS), F32)] + [((2, COLS, ROWS), BF)] * 3,
        [((3, COLS, ROWS), BF), ((COLS, ANC), F32), ((COLS, 4 * SEP), BF)],
        0,
        *(pos, low0, low1, load_whole("load_low", 2), upper, *[across[m] for m in (1, 2, 3)], y0, y1),
    )
    sol01 = add(outs[0], *[send_ring(outs[d], d) for d in (2, 1, 3)])
    ups = [send_xor(other, 1), send_xor(same, 8), send_xor(other, 9)]
    lower, higher = sol01[..., :SEP].astype(BF), sol01[..., SEP:].astype(BF)
    home, away = jnp.where(flip, higher, lower), jnp.where(flip, lower, higher)
    got = [send_xor(away, 1), send_xor(home, 8), send_xor(away, 9)]
    rest, anc_up = call(
        rest_kernel,
        "leaf_rest",
        "ssvvvvvvv:v",
        [((1024, 512), F32), ((3, SEP, 512), F32)],
        [((3 * SEP, 512), BF), ((1024, 3 * SEP), BF)],
        0,
        *(pos, pattern, leaf_rhs, leaf_inv, coup, same, *ups),
    )
    x_leaf, x_anc = call(
        final_kernel,
        "leaf_backward",
        "ssvvvvvvvv:a",
        [((1024, 512), F32), ((LEVELS, SEP, 512), F32)],
        [((2 * SEP, 512), BF), ((1024, 2 * SEP), BF), ((1024, 512), F32), ((2, SEP, 512), F32)],
        11,
        *(pos, pattern, leaf_inv, coup, sol01, *got, rest, anc_up),
    )
    return x_leaf, x_anc[None]


def solution(mesh):
    placed = (
        P(("layer", "row"), None),
        P(("layer", "row"), None, None),
        P(("layer", "row"), None, None),
        P(("layer", "row"), None),
        P("layer", None, "row", None),
        P("layer", None, "row", None),
    )
    return jax.shard_map(
        body,
        mesh=mesh,
        in_specs=placed,
        out_specs=(P(("layer", "row"), None), P("layer", None, "row", None)),
        check_vma=False,
    )
```
